256 devices in a mesh: dp: 32 (over y, z), tensor: 8 (over x, core).
Axes of the slice: x: 4, y: 4, z: 8, core: 2. Of those that a mesh axis runs over, the one named last changes fastest.
Arguments:
- text_states: bfloat16 [32, 256, 4096], P('dp'), may hold values from -6 to 6
- prompt_lengths: int32 [32], P('dp'), may hold values from 1 to 256, as said below
- attn_gain: float32 [4096], replicated, may hold values from 0.1 to 1.9
- query_w: bfloat16 [4096, 2048], P('dp', 'tensor'), may hold values from -0.25 to 0.25
- key_w: bfloat16 [4096, 2048], P('dp', 'tensor'), may hold values from -0.25 to 0.25
- value_w: bfloat16 [4096, 2048], P('dp', 'tensor'), may hold values from -0.09375 to 0.09375
- out_w: bfloat16 [2048, 4096], P('tensor', 'dp'), may hold values from -0.125 to 0.125
- context_w: bfloat16 [4096, 2432], P('tensor', 'dp'), may hold values from -0.09375 to 0.09375
- mod_scale: float32 [32, 2432], P('dp'), may hold values from -0.5 to 0.5
- mod_shift: float32 [32, 2432], P('dp'), may hold values from -5 to 5
- text_key_w: bfloat16 [2432, 1536], P('dp', 'tensor'), may hold values from -0.125 to 0.125
- text_value_w: bfloat16 [2432, 1536], P('dp', 'tensor'), may hold values from -0.125 to 0.125
- image_query: bfloat16 [32, 512, 1536], P('dp', 'tensor'), may hold values from -30 to 30
- image_key: bfloat16 [32, 512, 1536], P('dp', 'tensor'), may hold values from -30 to 30
- image_value: bfloat16 [32, 512, 1536], P('dp', 'tensor'), may hold values from -6 to 6
Outputs:
- image_mixed: bfloat16 [32, 512, 1536], P('dp', 'tensor')
The draws below stay inside these ranges and needn't reach their ends.
Inputs may be any that keep to these rules, and one draw needn't show every extreme that they name: `prompt_lengths`: some prompt has all 256 tokens in every draw.
All inputs are finite; a program needn't handle non-finite values.
Results may differ from the reference program's by a relative error of at most 0.015.
Values may be sent and summed in bfloat16 or wider, within the bound.
No kernel may reach another device: no remote copies, remote signals or barrier semaphores. Data moves between devices by JAX's collectives and lax.ppermute only.
A program may use at most 64 MiB of HBM per device.

```python
import math
import jax
import jax.numpy as jnp
from jax import lax

ENC = 4096
ENC_HEADS = 32
HEAD = 64
WIDTH = 2432
HEADS = 24
SLOTS = 256
LAT = 512
SAMPLES = 32
N_TENSOR = 8


def shared_normal(key, shape, limit):
    return jnp.clip(jax.random.normal(key, shape, jnp.float32), -limit, limit)


def draw_query_w(key, part):
    key = jax.random.fold_in(key, 11)
    own = 0.35 * shared_normal(key, (ENC, ENC_HEADS * HEAD), 6.0)
    return jnp.clip(own / math.sqrt(ENC), -0.25, 0.25).astype(jnp.bfloat16)


def draw_key_w(key, part):
    key = jax.random.fold_in(key, 12)
    own = 0.35 * shared_normal(key, (ENC, ENC_HEADS * HEAD), 6.0)
    return jnp.clip(own / math.sqrt(ENC), -0.25, 0.25).astype(jnp.bfloat16)


def draw_image_query(key, part):
    key = jax.random.fold_in(key, 21)
    own = shared_normal(key, (SAMPLES, LAT, HEADS * HEAD), 6.0)
    return own.astype(jnp.bfloat16)


def draw_image_key(key, part):
    key = jax.random.fold_in(key, 22)
    own = shared_normal(key, (SAMPLES, LAT, HEADS * HEAD), 6.0)
    return own.astype(jnp.bfloat16)


def draw_prompt_lengths(key, part):
    key = jax.random.fold_in(key, 31)
    first, second = jax.random.split(key)
    lengths = jax.random.randint(first, (SAMPLES,), 1, SLOTS + 1, jnp.int32)
    where = jax.random.randint(second, (), 0, SAMPLES, jnp.int32)
    return lengths.at[where].set(SLOTS)


def block_levels(rng, dims, shards, smallest, top_value):
    loudness = 1.0
    for position, parts in shards:
        draws = jax.random.uniform(jax.random.fold_in(jax.random.fold_in(rng, 6), position), (parts,), jnp.float32, smallest / len(shards), top_value / len(shards))
        loudness = loudness * jnp.repeat(jnp.exp(draws), dims[position] // parts).reshape((-1,) + (1,) * (len(dims) - 1 - position))
    return loudness


def centred(own_key, extent, scale, bound, cuts=(), dtype=jnp.bfloat16):
    array = scale * jax.random.normal(own_key, extent, jnp.float32)
    if cuts:
        array = array * block_levels(own_key, extent, cuts, -0.22, 0.18)
    return jnp.clip(array, -bound, bound).astype(dtype)


def setup_inputs(seed: int = 0) -> dict:
    splits = jax.random.split(jax.random.key(seed), 16)
    return {
        "text_states": centred(splits[0], (SAMPLES, SLOTS, ENC), 1.0, 6.0, ((0, 32),)),
        "prompt_lengths": draw_prompt_lengths(jax.random.fold_in(splits[15], 71), 0),
        "attn_gain": jnp.clip(1.0 + 0.18 * jax.random.normal(splits[2], (ENC,), jnp.float32), 0.1, 1.9),
        "query_w": draw_query_w(jax.random.fold_in(splits[15], 71), 0),
        "key_w": draw_key_w(jax.random.fold_in(splits[15], 71), 0),
        "value_w": centred(splits[5], (ENC, ENC_HEADS * HEAD), ENC ** -0.5, 0.09375, ((0, 32), (1, 8))),
        "out_w": centred(splits[6], (ENC_HEADS * HEAD, ENC), (ENC_HEADS * HEAD) ** -0.5, 0.125, ((0, 8), (1, 32))),
        "context_w": centred(splits[7], (ENC, WIDTH), ENC ** -0.5, 0.09375, ((0, 8), (1, 32))),
        "mod_scale": jnp.clip(jax.random.uniform(splits[8], (SAMPLES, WIDTH), jnp.float32, -0.5, 0.5) * block_levels(splits[8], (SAMPLES, WIDTH), ((0, 32),), -0.4, 0.0), -0.5, 0.5),
        "mod_shift": centred(splits[9], (SAMPLES, WIDTH), 1.0, 5.0, ((0, 32),), jnp.float32),
        "text_key_w": centred(splits[10], (WIDTH, HEADS * HEAD), WIDTH ** -0.5, 0.125, ((0, 32), (1, 8))),
        "text_value_w": centred(splits[11], (WIDTH, HEADS * HEAD), WIDTH ** -0.5, 0.125, ((0, 32), (1, 8))),
        "image_query": draw_image_query(jax.random.fold_in(splits[15], 71), 0),
        "image_key": draw_image_key(jax.random.fold_in(splits[15], 71), 0),
        "image_value": centred(splits[14], (SAMPLES, LAT, HEADS * HEAD), 1.0, 6.0, ((0, 32), (1, 8))),
    }


EPS = 1e-06

def rms_scale(values, gain):
    return values * lax.rsqrt(lax.optimization_barrier(jnp.mean(values * values, axis=-1, keepdims=True)) + EPS) * gain

def masked_softmax(scores, valid):
    scores = jnp.where(valid, scores, -jnp.inf)
    top = lax.optimization_barrier(jnp.max(scores, axis=-1, keepdims=True))
    expo = jnp.exp(scores - top)
    return (expo, lax.optimization_barrier(jnp.sum(expo, axis=-1, keepdims=True)))

def rounded_sum(partial_value):
    rounded = lax.optimization_barrier(partial_value.astype(jnp.bfloat16))
    return lax.optimization_barrier(jnp.sum(rounded.astype(jnp.float32), axis=0))

def reference(text_states, prompt_lengths, attn_gain, query_w, key_w, value_w, out_w, context_w, mod_scale, mod_shift, text_key_w, text_value_w, image_query, image_key, image_value):
    enc_block = ENC_HEADS * HEAD // N_TENSOR
    feature_block = ENC // N_TENSOR
    out_blocks = out_w.astype(jnp.float32).reshape(N_TENSOR, enc_block, ENC)
    context_blocks = context_w.astype(jnp.float32).reshape(N_TENSOR, feature_block, WIDTH)

    def one_sample(items):
        text_row, length, scale_row, shift_row, query_row, key_row, value_row = items
        states = text_row.astype(jnp.float32)
        normed = rms_scale(states, attn_gain).astype(jnp.bfloat16)

        def project(weight):
            product = jnp.dot(normed, weight, preferred_element_type=jnp.float32)
            return product.astype(jnp.bfloat16).reshape(SLOTS, ENC_HEADS, HEAD)
        enc_q = project(query_w)
        enc_k = project(key_w)
        enc_v = project(value_w)
        scores = jnp.einsum('qhd,khd->hqk', enc_q.astype(jnp.float32), enc_k.astype(jnp.float32))
        valid = (lax.iota(jnp.int32, SLOTS) < length)[None, None, :]
        expo, total = masked_softmax(scores, valid)
        mixed = jnp.einsum('hqk,khd->qhd', expo.astype(jnp.bfloat16).astype(jnp.float32), enc_v.astype(jnp.float32))
        mixed = (mixed / jnp.transpose(total, (1, 0, 2))).astype(jnp.bfloat16)
        grouped = mixed.reshape(SLOTS, N_TENSOR, enc_block).astype(jnp.float32)
        attn = rounded_sum(jnp.einsum('snb,nbe->nse', grouped, out_blocks))
        embedded = (states + attn).astype(jnp.bfloat16)
        pieces = embedded.reshape(SLOTS, N_TENSOR, feature_block).astype(jnp.float32)
        context = rounded_sum(jnp.einsum('snb,nbw->nsw', pieces, context_blocks))
        centered = context - lax.optimization_barrier(jnp.mean(context, axis=-1, keepdims=True))
        spread = lax.optimization_barrier(jnp.mean(centered * centered, axis=-1, keepdims=True))
        modulated = (centered * lax.rsqrt(spread + EPS) * (1.0 + scale_row) + shift_row).astype(jnp.bfloat16)
        text_k = jnp.dot(modulated, text_key_w, preferred_element_type=jnp.float32).astype(jnp.bfloat16)
        text_v = jnp.dot(modulated, text_value_w, preferred_element_type=jnp.float32).astype(jnp.bfloat16)
        all_keys = jnp.concatenate([key_row, text_k], axis=0).reshape(LAT + SLOTS, HEADS, HEAD)
        all_values = jnp.concatenate([value_row, text_v], axis=0).reshape(LAT + SLOTS, HEADS, HEAD)
        queries = query_row.reshape(LAT, HEADS, HEAD)
        joint = jnp.einsum('qhd,khd->hqk', queries.astype(jnp.float32), all_keys.astype(jnp.float32)) * HEAD ** (-0.5)
        slot_ok = jnp.concatenate([lax.iota(jnp.int32, LAT) >= 0, lax.iota(jnp.int32, SLOTS) < length])
        joint_exp, joint_total = masked_softmax(joint, slot_ok[None, None, :])
        result = jnp.einsum('hqk,khd->qhd', joint_exp.astype(jnp.bfloat16).astype(jnp.float32), all_values.astype(jnp.float32))
        result = result / jnp.transpose(joint_total, (1, 0, 2))
        return result.astype(jnp.bfloat16).reshape(LAT, HEADS * HEAD)
    return lax.map(one_sample, (text_states, prompt_lengths, mod_scale, mod_shift, image_query, image_key, image_value))
```

```python
import jax
import jax.numpy as jnp
from jax import lax
from jax.sharding import Mesh
from jax.sharding import PartitionSpec as P

HEAD = 64
EPS = 1e-06
NY, NZ, NX, NC = 4, 8, 4, 2
DP = ("y", "z")
TENSOR = ("x", "c")
WIDTH = 2432
PIECE = 76
PADDED = 80
BF = jnp.bfloat16
F32 = jnp.float32


def shift(array, axis, size, step):
    return lax.ppermute(array, axis, [(i, (i + step) % size) for i in range(size)])


def ring_z(block):
    forward = backward = block
    found = [(0, block)]
    for step in range(1, 5):
        forward = shift(forward, "z", NZ, 1)
        found.append((-step, forward))
        if step < 4:
            backward = shift(backward, "z", NZ, -1)
            found.append((step, backward))
    return found


def share_y(block):
    return lax.all_to_all(
        jnp.broadcast_to(block[None], (NY,) + block.shape), "y", 0, 0, tiled=True
    )


def gather_z_first(shard):
    z = lax.axis_index("z")
    line = jnp.zeros((NZ,) + shard.shape, shard.dtype)
    for step, piece in ring_z(shard):
        line = lax.dynamic_update_slice_in_dim(line, piece[None], (z + step) % NZ, 0)
    return share_y(line)


def gather_y_first(shard):
    z = lax.axis_index("z")
    block = share_y(shard)
    plane = jnp.zeros((NY, NZ) + shard.shape, shard.dtype)
    for step, piece in ring_z(block):
        plane = lax.dynamic_update_slice_in_dim(plane, piece[:, None], (z + step) % NZ, 1)
    return plane


def lane_blocks(array):
    return [array[:, i : i + 128] for i in range(0, array.shape[1], 128)]


def masked_softmax(scores, valid):
    scores = jnp.where(valid, scores, -jnp.inf)
    top = jnp.max(scores, axis=-1, keepdims=True)
    expo = jnp.exp(scores - top)
    return (expo, jnp.sum(expo, axis=-1, keepdims=True))


def tensor_exchange(array):
    return lax.all_to_all(array, TENSOR, 0, 0, tiled=True)


def per_device(
    text_states,
    prompt_lengths,
    attn_gain,
    query_w,
    key_w,
    value_w,
    out_w,
    context_w,
    mod_scale,
    mod_shift,
    text_key_w,
    text_value_w,
    image_query,
    image_key,
    image_value,
):
    slots, enc = text_states.shape[1:]
    ndev = NX * NC
    me = lax.axis_index("x") * NC + lax.axis_index("c")
    pad_rows = ((0, PADDED - PIECE), (0, 0))
    context_t = jnp.pad(context_w.T, pad_rows)
    text_w = jnp.pad(jnp.concatenate([text_key_w, text_value_w], axis=1), pad_rows)
    packed = jnp.concatenate([out_w] + lane_blocks(context_t) + lane_blocks(text_w), axis=0)
    gathered = lax.all_gather(packed, DP, axis=0)

    qkv = jnp.concatenate([query_w, key_w, value_w], axis=1)
    half = qkv.shape[1] // 2
    w_b = gather_y_first(qkv[:, half:]).reshape(enc, half)
    w_a = gather_z_first(qkv[:, :half]).reshape(enc, half)

    flat = text_states[0].astype(F32)
    scale = lax.rsqrt(jnp.mean(flat * flat, axis=-1, keepdims=True) + EPS)
    normed = (flat * scale * attn_gain).astype(BF)

    nheads = image_query.shape[-1] // HEAD // ndev
    local = nheads * HEAD
    tokens = image_query.shape[1]
    image = jnp.concatenate(
        [
            jnp.swapaxes(part[0].reshape(tokens, ndev, local), 0, 1)
            for part in (image_query, image_key, image_value)
        ],
        axis=-1,
    )
    image = tensor_exchange(image).reshape(ndev * tokens, 3 * local)

    part_b = jnp.dot(normed, w_b, preferred_element_type=F32).astype(BF)
    part_a = jnp.dot(normed, w_a, preferred_element_type=F32).astype(BF)
    enc_all = jnp.concatenate([part_a, part_b], axis=1)
    width = query_w.shape[1]
    heads = width // HEAD
    enc_q, enc_k, enc_v = (
        enc_all[:, i * width : (i + 1) * width].reshape(slots, heads, HEAD) for i in range(3)
    )
    text_ok = lax.iota(jnp.int32, slots) < prompt_lengths[0]
    scores = jnp.einsum("qhd,khd->hqk", enc_q, enc_k, preferred_element_type=F32)
    expo, total = masked_softmax(scores, text_ok[None, None, :])
    mixed = jnp.einsum("hqk,khd->qhd", expo.astype(BF), enc_v, preferred_element_type=F32)
    mixed = (mixed / jnp.swapaxes(total, 0, 1)).astype(BF).reshape(slots, width)

    rows = out_w.shape[0]
    out_all = jnp.swapaxes(gathered[:, :rows], 0, 1).reshape(rows, enc)
    attn_part = jnp.dot(mixed, out_all, preferred_element_type=F32).astype(BF)
    share = enc // ndev
    attn_parts = tensor_exchange(jnp.swapaxes(attn_part.reshape(slots, ndev, share), 0, 1))
    attn = jnp.sum(attn_parts.astype(F32), axis=0)
    mine = lax.dynamic_slice_in_dim(text_states[0], me * share, share, 1)
    embedded = (mine.astype(F32) + attn).astype(BF)

    c_rows = PADDED * share // 128
    wide = NY * NZ * PADDED
    context_all = gathered[:, rows : rows + c_rows].reshape(NY * NZ, share // 128, PADDED, 128)
    context_all = jnp.swapaxes(context_all, 1, 2).reshape(wide, share)
    context_part = lax.dot_general(
        embedded, context_all, (((1,), (1,)), ((), ())), preferred_element_type=F32
    ).astype(BF)
    context = tensor_exchange(context_part.reshape(ndev, slots // ndev, wide))
    context = jnp.sum(context.astype(F32), axis=0)
    real = jnp.tile(lax.iota(jnp.int32, PADDED) < PIECE, NY * NZ)
    centered = jnp.where(real, context - jnp.sum(context, axis=-1, keepdims=True) / WIDTH, 0.0)
    spread = jnp.sum(centered * centered, axis=-1, keepdims=True) / WIDTH

    def spaced(row):
        return jnp.pad(row.reshape(NY * NZ, PIECE), ((0, 0), (0, PADDED - PIECE))).reshape(1, wide)

    modulated = centered * lax.rsqrt(spread + EPS) * (1.0 + spaced(mod_scale)) + spaced(mod_shift)
    modulated = modulated.astype(BF)
    modulated = tensor_exchange(jnp.broadcast_to(modulated[None], (ndev,) + modulated.shape))
    modulated = modulated.reshape(slots, wide)

    text_all = gathered[:, rows + c_rows :].reshape(NY * NZ, 2 * local // 128, PADDED, 128)
    text_all = jnp.swapaxes(text_all, 1, 2).reshape(wide, 2 * local)
    text_kv = jnp.dot(modulated, text_all, preferred_element_type=F32).astype(BF)

    def by_head(array):
        return array.reshape(array.shape[0], nheads, HEAD)

    query = by_head(image[:, :local])
    keys = by_head(jnp.concatenate([image[:, local : 2 * local], text_kv[:, :local]], axis=0))
    values = by_head(jnp.concatenate([image[:, 2 * local :], text_kv[:, local:]], axis=0))
    ok = jnp.concatenate([jnp.ones((ndev * tokens,), bool), text_ok])
    scores = jnp.einsum("qhd,khd->hqk", query, keys, preferred_element_type=F32) * HEAD ** (-0.5)
    expo, total = masked_softmax(scores, ok[None, None, :])
    result = jnp.einsum("hqk,khd->qhd", expo.astype(BF), values, preferred_element_type=F32)
    result = (result / jnp.swapaxes(total, 0, 1)).astype(BF).reshape(ndev, tokens, local)
    result = tensor_exchange(result)
    return jnp.swapaxes(result, 0, 1).reshape(1, tokens, ndev * local)


def solution(mesh):
    fine = Mesh(mesh.devices.reshape(NY, NZ, NX, NC), DP + TENSOR)
    in_specs = (
        P(DP, None, None),
        P(DP),
        P(),
        P(DP, TENSOR),
        P(DP, TENSOR),
        P(DP, TENSOR),
        P(TENSOR, DP),
        P(TENSOR, DP),
        P(DP, None),
        P(DP, None),
        P(DP, TENSOR),
        P(DP, TENSOR),
        P(DP, TENSOR, None),
        P(DP, TENSOR, None),
        P(DP, TENSOR, None),
    )
    out_specs = P(DP, TENSOR, None)
    return jax.shard_map(
        per_device, mesh=fine, in_specs=in_specs, out_specs=out_specs, check_vma=False
    )
```

```python
import functools

import jax
import jax.numpy as jnp
from jax import lax
from jax.experimental import pallas as pl
from jax.experimental.pallas import tpu as pltpu
from jax.sharding import Mesh
from jax.sharding import PartitionSpec as P

HEAD = 64
EPS = 1e-06
NY, NZ, NX, NC = 4, 8, 4, 2
DP = ("y", "z")
TENSOR = ("x", "c")
WIDTH = 2432
PIECE = 76
PADDED = 80
BF = jnp.bfloat16
F32 = jnp.float32


def shift(array, axis, size, step):
    return lax.ppermute(array, axis, [(i, (i + step) % size) for i in range(size)])


def gather_weights(shard, later):
    half = shard.shape[0] // 2
    y = lax.axis_index("y")

    def z_pair(ahead, behind):
        return shift(ahead, "z", NZ, 1), shift(behind, "z", NZ, -1)

    up, down = shift(shard, "y", NY, 1), shift(shard, "y", NY, -1)
    far = [shift(up[:half], "y", NY, 1), shift(down[half:], "y", NY, -1)]
    far = jnp.concatenate(far, axis=0)
    block = jnp.zeros((NY,) + shard.shape, shard.dtype)
    for step, piece in ((0, shard), (-1, up), (1, down), (2, far)):
        block = lax.dynamic_update_slice_in_dim(block, piece[None], (y + step) % NY, 0)
    block, *later = lax.optimization_barrier((block, *later))
    s1, t1 = z_pair(block, block)
    s2, t2 = z_pair(s1, t1)
    s3, t3 = z_pair(s2, t2)
    s4 = shift(s3[: NY // 2], "z", NZ, 1)
    t4 = shift(t3[NY // 2 :], "z", NZ, -1)
    last = jnp.concatenate([s4, t4], axis=0)
    ring = [(0, block), (-1, s1), (1, t1), (-2, s2), (2, t2), (-3, s3), (3, t3), (4, last)]
    return ring, later


def encoder_kernel(
    heads, steps, length_ref, states_ref, qk_w_ref, v_ref, out_w_ref, out_ref, qk_ref, mixed_ref
):
    i = pl.program_id(0)
    width = heads * HEAD
    depth = qk_w_ref.shape[2]

    @pl.when(i == 0)
    def _():
        qk_ref[...] = jnp.zeros_like(qk_ref)

    @pl.when(i < steps)
    def _():
        weights = [
            jnp.concatenate([qk_w_ref[k, n : n + depth] for n in range(0, 2 * width, depth)], axis=1)
            for k in range(qk_w_ref.shape[0])
        ]
        qk_ref[...] += jnp.dot(
            states_ref[...], jnp.concatenate(weights, axis=0), preferred_element_type=F32
        )

    @pl.when(i == steps - 1)
    def _():
        slots = qk_ref.shape[0]
        ok = lax.broadcasted_iota(jnp.int32, (slots, slots), 1) < length_ref[0]
        for h in range(heads):
            cols = slice(h * HEAD, (h + 1) * HEAD)
            query = qk_ref[:, cols].astype(BF)
            key = qk_ref[:, width + h * HEAD : width + (h + 1) * HEAD].astype(BF)
            scores = lax.dot_general(
                query, key, (((1,), (1,)), ((), ())), preferred_element_type=F32
            )
            scores = jnp.where(ok, scores, -jnp.inf)
            expo = jnp.exp(scores - jnp.max(scores, axis=-1, keepdims=True))
            total = jnp.sum(expo, axis=-1, keepdims=True)
            mixed = jnp.dot(expo.astype(BF), v_ref[:, cols], preferred_element_type=F32)
            mixed_ref[:, cols] = (mixed / total).astype(BF)

    @pl.when(i >= steps)
    def _():
        for k in range(out_ref.shape[0]):
            out_ref[k] = jnp.dot(
                mixed_ref[...], out_w_ref[k], preferred_element_type=F32
            ).astype(BF)


def encoder(length, states, gathered, row, v, w_out):
    slots, width = v.shape
    pieces, rows, cols = w_out.shape
    shard = states.shape[1] // pieces
    at_once, steps = 4, pieces // 4
    out_at_once = 8

    def early(i):
        return jnp.minimum(i, steps - 1)

    def late(i):
        return jnp.maximum(i - steps, 0)

    return pl.pallas_call(
        functools.partial(encoder_kernel, width // HEAD, steps),
        grid=(steps + pieces // out_at_once,),
        in_specs=[
            pl.BlockSpec(memory_space=pltpu.SMEM),
            pl.BlockSpec((slots, at_once * shard), lambda i: (0, early(i))),
            pl.BlockSpec(
                (pl.Element(at_once), pl.Element(2 * width // 128 * shard), pl.Element(128)),
                lambda i: (early(i) * at_once, row, 0),
            ),
            pl.BlockSpec(v.shape, lambda i: (0, 0)),
            pl.BlockSpec((out_at_once, rows, cols), lambda i: (late(i), 0, 0)),
        ],
        out_specs=pl.BlockSpec((out_at_once, slots, cols), lambda i: (late(i), 0, 0)),
        out_shape=jax.ShapeDtypeStruct((pieces, slots, cols), BF),
        scratch_shapes=[pltpu.VMEM((slots, 2 * width), F32), pltpu.VMEM((slots, width), BF)],
        compiler_params=pltpu.CompilerParams(vmem_limit_bytes=40 * 2**20),
        cost_estimate=pl.CostEstimate(
            flops=2 * slots * (rows * pieces * cols + 2 * width * pieces * shard),
            bytes_accessed=pieces * 2 * (cols * (rows + slots) + shard * (slots + 2 * width)),
            transcendentals=slots * slots * width // HEAD,
        ),
    )(length, states, gathered, v, w_out)


def context_kernel(embedded_ref, weights_ref, out_ref):
    for k in range(weights_ref.shape[0]):
        total = 0
        for n in range(embedded_ref.shape[0]):
            total += lax.dot_general(
                weights_ref[k, n * PADDED : (n + 1) * PADDED],
                embedded_ref[n],
                (((1,), (1,)), ((), ())),
                preferred_element_type=F32,
            )
        out_ref[k] = total.astype(BF)


def embed_context(embedded, gathered, row):
    blocks, slots, _ = embedded.shape
    pieces = gathered.shape[0]
    at_once = 8
    return pl.pallas_call(
        context_kernel,
        grid=(pieces // at_once,),
        in_specs=[
            pl.BlockSpec(embedded.shape, lambda i: (0, 0, 0)),
            pl.BlockSpec(
                (pl.Element(at_once), pl.Element(blocks * PADDED), pl.Element(128)),
                lambda i: (i * at_once, row, 0),
            ),
        ],
        out_specs=pl.BlockSpec((at_once, PADDED, slots), lambda i: (i, 0, 0)),
        out_shape=jax.ShapeDtypeStruct((pieces, PADDED, slots), BF),
        compiler_params=pltpu.CompilerParams(vmem_limit_bytes=40 * 2**20),
        cost_estimate=pl.CostEstimate(
            flops=2 * pieces * PADDED * blocks * 128 * slots,
            bytes_accessed=pieces * PADDED * 2 * (blocks * 128 + slots),
            transcendentals=0,
        ),
    )(embedded, gathered)


def joint_kernel(
    row, length_ref, context_ref, scale_ref, shift_ref, image_ref, gathered_ref, out_ref, text_ref, sem
):
    pieces, rows, slots = context_ref.shape
    cols = text_ref.shape[1] // rows
    local = out_ref.shape[1]
    copy = pltpu.make_async_copy(
        gathered_ref.at[:, pl.ds(row, cols * rows)], text_ref, sem.at[0]
    )
    copy.start()
    real = lax.broadcasted_iota(jnp.int32, (rows, slots), 0) < PIECE
    total = jnp.zeros((rows, slots), F32)
    for k in range(pieces):
        total += context_ref[k].astype(F32)
    mean = jnp.sum(total, axis=0, keepdims=True) / WIDTH
    square = jnp.zeros((rows, slots), F32)
    for k in range(pieces):
        centered = context_ref[k].astype(F32) - mean
        square += centered * centered
    square = jnp.where(real, square, 0.0)
    factor = lax.rsqrt(jnp.sum(square, axis=0, keepdims=True) / WIDTH + EPS)
    copy.wait()
    text = jnp.zeros((cols * 128, slots), F32)
    for k in range(pieces):
        scale = 1.0 + jnp.concatenate([scale_ref[k]] * (slots // 128), axis=1)
        move = jnp.concatenate([shift_ref[k]] * (slots // 128), axis=1)
        modulated = (context_ref[k].astype(F32) - mean) * factor * scale + move
        modulated = jnp.where(real, modulated, 0.0).astype(BF)
        weights = [text_ref[k, n * rows : (n + 1) * rows] for n in range(cols)]
        text += lax.dot_general(
            jnp.concatenate(weights, axis=1),
            modulated,
            (((0,), (0,)), ((), ())),
            preferred_element_type=F32,
        )
    text = text.astype(BF)
    tokens = image_ref.shape[0]
    ok = lax.broadcasted_iota(jnp.int32, (tokens, slots), 1) < length_ref[0]
    for h in range(local // HEAD):
        at = h * HEAD
        query = image_ref[:, at : at + HEAD]
        key = image_ref[:, local + at : local + at + HEAD]
        value = image_ref[:, 2 * local + at : 2 * local + at + HEAD]
        near = lax.dot_general(query, key, (((1,), (1,)), ((), ())), preferred_element_type=F32)
        near = near * HEAD ** (-0.5)
        far = jnp.dot(query, text[at : at + HEAD], preferred_element_type=F32) * HEAD ** (-0.5)
        far = jnp.where(ok, far, -jnp.inf)
        top = jnp.maximum(
            jnp.max(near, axis=-1, keepdims=True), jnp.max(far, axis=-1, keepdims=True)
        )
        near, far = jnp.exp(near - top), jnp.exp(far - top)
        sums = jnp.sum(near, axis=-1, keepdims=True) + jnp.sum(far, axis=-1, keepdims=True)
        result = jnp.dot(near.astype(BF), value, preferred_element_type=F32)
        result += lax.dot_general(
            far.astype(BF),
            text[local + at : local + at + HEAD],
            (((1,), (1,)), ((), ())),
            preferred_element_type=F32,
        )
        out_ref[:, at : at + HEAD] = (result / sums).astype(BF)


def joint(length, context, scale, move, image, gathered, row):
    pieces, rows, slots = context.shape
    tokens, cols = image.shape
    text_rows = gathered.shape[1] - row
    vmem = pl.BlockSpec(memory_space=pltpu.VMEM)
    return pl.pallas_call(
        functools.partial(joint_kernel, row),
        in_specs=[pl.BlockSpec(memory_space=pltpu.SMEM)]
        + [vmem] * 4
        + [pl.BlockSpec(memory_space=pl.ANY)],
        out_specs=vmem,
        out_shape=jax.ShapeDtypeStruct((tokens, cols // 3), BF),
        scratch_shapes=[
            pltpu.VMEM((pieces, text_rows, 128), BF),
            pltpu.SemaphoreType.DMA((1,)),
        ],
        compiler_params=pltpu.CompilerParams(vmem_limit_bytes=48 * 2**20),
        cost_estimate=pl.CostEstimate(
            flops=2 * pieces * rows * text_rows // rows * 128 * slots
            + 4 * tokens * (tokens + slots) * cols // 3,
            bytes_accessed=pieces * rows * 2 * (slots + text_rows // rows * 128),
            transcendentals=tokens * (tokens + slots) * cols // 3 // HEAD,
        ),
    )(length, context, scale, move, image, gathered)


def lane_blocks(array):
    return [array[:, i : i + 128] for i in range(0, array.shape[1], 128)]


def tensor_exchange(array):
    return lax.all_to_all(array, TENSOR, 0, 0, tiled=True)


def take(array, index, axis=0):
    return lax.dynamic_index_in_dim(array, index, axis, keepdims=False)


def other_core(array):
    return shift(array, "c", NC, 1)


def reduce_tensor(parts):
    x, c = lax.axis_index("x"), lax.axis_index("c")
    parts = parts.reshape((NX, NC) + parts.shape[1:])
    received = other_core(take(parts, 1 - c, 1))
    chip = (take(parts, c, 1).astype(F32) + received.astype(F32)).astype(parts.dtype)
    near = [shift(take(chip, (x + d) % NX), "x", NX, d) for d in (1, -1)]
    far = take(chip, (x + 2) % NX)
    half = far.shape[0] // 2
    far = [shift(far[:half], "x", NX, 2), shift(far[half:], "x", NX, -2)]
    far = jnp.concatenate(far, axis=0)
    total = take(chip, x).astype(F32) + near[0].astype(F32)
    return total + near[1].astype(F32) + far.astype(F32)


def gather_tensor(block):
    x, c = lax.axis_index("x"), lax.axis_index("c")
    line = jnp.zeros((NX,) + block.shape, block.dtype)
    pieces = [(0, block)] + [(-d, shift(block, "x", NX, d)) for d in (1, -1, 2)]
    for step, piece in pieces:
        line = lax.dynamic_update_slice_in_dim(line, piece[None], (x + step) % NX, 0)
    other = other_core(line)
    low, high = jnp.where(c == 0, line, other), jnp.where(c == 0, other, line)
    return jnp.stack([low, high], axis=1)


def per_device(
    text_states,
    prompt_lengths,
    attn_gain,
    query_w,
    key_w,
    value_w,
    out_w,
    context_w,
    mod_scale,
    mod_shift,
    text_key_w,
    text_value_w,
    image_query,
    image_key,
    image_value,
):
    slots, enc = text_states.shape[1:]
    ndev = NX * NC
    pieces = NY * NZ
    me = lax.axis_index("x") * NC + lax.axis_index("c")
    width = query_w.shape[1]
    shard = query_w.shape[0]
    share = enc // ndev
    pad_rows = ((0, PADDED - PIECE), (0, 0))
    context_t = jnp.pad(context_w.T, pad_rows)
    text_w = jnp.pad(jnp.concatenate([text_key_w, text_value_w], axis=1), pad_rows)
    parts = [lane_blocks(w) for w in (query_w, key_w, context_t, text_w)]
    packed = jnp.concatenate(sum(parts, []), axis=0)
    context_row = 2 * width // 128 * shard
    text_row = context_row + share // 128 * PADDED
    out_rows = jnp.concatenate([out_w[:shard], out_w[shard:]], axis=1)
    second = jnp.concatenate([value_w, out_rows], axis=0)
    packed, second = lax.optimization_barrier((packed, second))
    gathered = lax.all_gather(packed, DP, axis=0)
    later = (text_states, image_query, image_key, image_value)
    ring, later = gather_weights(second, later)
    text_states, image_query, image_key, image_value = later

    flat = text_states[0].astype(F32)
    scale = lax.rsqrt(jnp.mean(flat * flat, axis=-1, keepdims=True) + EPS)
    normed = (flat * scale * attn_gain).astype(BF)

    nheads = image_query.shape[-1] // HEAD // ndev
    local = nheads * HEAD
    tokens = image_query.shape[1]
    image = jnp.concatenate(
        [
            jnp.swapaxes(part[0].reshape(tokens, ndev, local), 0, 1)
            for part in (image_query, image_key, image_value)
        ],
        axis=-1,
    )
    image = tensor_exchange(image).reshape(ndev * tokens, 3 * local)

    z = lax.axis_index("z")
    v_all = jnp.zeros((NY, NZ, shard, width), BF)
    w_out = jnp.zeros((NY, NZ, 2 * shard, shard), BF)
    for step, piece in ring:
        at = (z + step) % NZ
        v_all = lax.dynamic_update_slice_in_dim(v_all, piece[:, None, :shard], at, 1)
        rows = jnp.concatenate([piece[:, shard:, :128], piece[:, shard:, 128:]], axis=1)
        w_out = lax.dynamic_update_slice_in_dim(w_out, rows[:, None], at, 1)
    w_out = w_out.reshape(pieces, 2 * shard, shard)
    enc_v = jnp.dot(normed, v_all.reshape(enc, width), preferred_element_type=F32).astype(BF)

    def spaced(row):
        row = jnp.pad(row.reshape(pieces, PIECE), ((0, 0), (0, PADDED - PIECE)))
        return jnp.broadcast_to(row[:, :, None], (pieces, PADDED, 128))

    scale, move = spaced(mod_scale), spaced(mod_shift)
    mine = lax.dynamic_slice_in_dim(text_states[0], me * share, share, 1).astype(F32)
    mine = jnp.swapaxes(mine.reshape(slots, share // 128, 128), 0, 1)
    ready = lax.optimization_barrier((enc_v, image, w_out, scale, move, mine))
    enc_v, image, w_out, scale, move, mine = ready

    attn_part = encoder(prompt_lengths, normed, gathered, 0, enc_v, w_out)
    attn = reduce_tensor(attn_part.reshape(ndev, share // 128 * slots, 128))
    embedded = (mine + attn.reshape(mine.shape)).astype(BF)
    context_part = embed_context(embedded, gathered, context_row)
    context = reduce_tensor(context_part.reshape(ndev, pieces // ndev * PADDED, slots))
    context = gather_tensor(context.astype(BF)).reshape(pieces, PADDED, slots)
    result = joint(prompt_lengths, context, scale, move, image, gathered, text_row)
    result = tensor_exchange(result.reshape(ndev, tokens, local))
    return jnp.swapaxes(result, 0, 1).reshape(1, tokens, ndev * local)


def solution(mesh):
    fine = Mesh(mesh.devices.reshape(NY, NZ, NX, NC), DP + TENSOR)
    in_specs = (
        P(DP, None, None),
        P(DP),
        P(),
        P(DP, TENSOR),
        P(DP, TENSOR),
        P(DP, TENSOR),
        P(TENSOR, DP),
        P(TENSOR, DP),
        P(DP, None),
        P(DP, None),
        P(DP, TENSOR),
        P(DP, TENSOR),
        P(DP, TENSOR, None),
        P(DP, TENSOR, None),
        P(DP, TENSOR, None),
    )
    out_specs = P(DP, TENSOR, None)
    return jax.shard_map(
        per_device, mesh=fine, in_specs=in_specs, out_specs=out_specs, check_vma=False
    )
```

```python
import functools

import jax
import jax.numpy as jnp
from jax import lax
from jax.experimental import pallas as pl
from jax.experimental.pallas import tpu as pltpu
from jax.sharding import Mesh
from jax.sharding import PartitionSpec as P

HEAD = 64
EPS = 1e-06
NY, NZ, NX, NC = 4, 8, 4, 2
DP = ("y", "z")
TENSOR = ("x", "c")
WIDTH = 2432
PIECE = 76
PADDED = 80
BF = jnp.bfloat16
F32 = jnp.float32
BIG = 56 * 2**20


def shift(array, axis, size, step):
    return lax.ppermute(array, axis, [(i, (i + step) % size) for i in range(size)])


def gather_over_y(shard):
    half = shard.shape[0] // 2
    y = lax.axis_index("y")
    up, down = shift(shard, "y", NY, 1), shift(shard, "y", NY, -1)
    far = [shift(up[:half], "y", NY, 1), shift(down[half:], "y", NY, -1)]
    far = jnp.concatenate(far, axis=0)
    block = jnp.zeros((NY,) + shard.shape, shard.dtype)
    for step, piece in ((0, shard), (-1, up), (1, down), (2, far)):
        block = lax.dynamic_update_slice_in_dim(block, piece[None], (y + step) % NY, 0)
    return block


def ring_over_z(block):
    def z_pair(ahead, behind):
        return shift(ahead, "z", NZ, 1), shift(behind, "z", NZ, -1)

    s1, t1 = z_pair(block, block)
    s2, t2 = z_pair(s1, t1)
    s3, t3 = z_pair(s2, t2)
    s4 = shift(s3[: NY // 2], "z", NZ, 1)
    t4 = shift(t3[NY // 2 :], "z", NZ, -1)
    last = jnp.concatenate([s4, t4], axis=0)
    return [(0, block), (-1, s1), (1, t1), (-2, s2), (2, t2), (-3, s3), (3, t3), (4, last)]


def place_z(ring, split):
    z = lax.axis_index("z")
    pieces = [(step, split(block)) for step, block in ring]
    whole = jnp.zeros((NY, NZ) + pieces[0][1].shape[1:], pieces[0][1].dtype)
    for step, piece in pieces:
        whole = lax.dynamic_update_slice_in_dim(whole, piece[:, None], (z + step) % NZ, 1)
    return whole


def columns_to_devices(out_w):
    pairs = []
    for y in range(NY):
        for z in range(NZ):
            for x in range(NX):
                for c in range(NC):
                    source = ((x * NZ + 4 * c + z // 2) * NX + y) * NC + z % 2
                    pairs.append((source, ((y * NZ + z) * NX + x) * NC + c))
    return lax.ppermute(out_w, DP + TENSOR, pairs)


def pack_kernel(query_ref, key_ref, context_ref, key_w_ref, value_w_ref, out_ref, text_ref, spare_ref, flat_ref):
    shard = query_ref.shape[0]
    row = 0
    for ref in (query_ref, key_ref):
        for n in range(0, ref.shape[1], 128):
            out_ref[row : row + shard] = ref[:, n : n + 128]
            row += shard
    spare_ref[...] = jnp.zeros_like(spare_ref)
    spare_ref[:, :PIECE] = context_ref[...].astype(F32)
    for n in range(0, spare_ref.shape[0], 128):
        turned = spare_ref[n : n + 128].T
        out_ref[row : row + PADDED] = turned[:PADDED].astype(BF)
        row += PADDED
    flat_ref[...] = jnp.zeros_like(flat_ref)
    local = key_w_ref.shape[1]
    flat_ref[:PIECE, :local] = key_w_ref[...].astype(F32)
    flat_ref[:PIECE, local:] = value_w_ref[...].astype(F32)
    text_ref[...] = flat_ref[...].astype(BF)


def pack(query_w, key_w, context_w, text_key_w, text_value_w):
    rows = 2 * query_w.shape[0] * query_w.shape[1] // 128 + context_w.shape[0] // 128 * PADDED
    cols = 2 * text_key_w.shape[1]
    vmem = pl.BlockSpec(memory_space=pltpu.VMEM)
    return pl.pallas_call(
        pack_kernel,
        in_specs=[vmem] * 5,
        out_specs=[vmem] * 2,
        out_shape=[
            jax.ShapeDtypeStruct((rows, 128), BF),
            jax.ShapeDtypeStruct((PADDED, cols), BF),
        ],
        scratch_shapes=[
            pltpu.VMEM((context_w.shape[0], 128), F32),
            pltpu.VMEM((PADDED, cols), F32),
        ],
        compiler_params=pltpu.CompilerParams(vmem_limit_bytes=40 * 2**20),
    )(query_w, key_w, context_w, text_key_w, text_value_w)


def encoder_kernel(heads, length_ref, states_ref, qk_w_ref, v_ref, out_ref, qk_ref):
    i = pl.program_id(0)
    width = heads * HEAD
    depth = qk_w_ref.shape[1] * 128 // (2 * width)

    @pl.when(i == 0)
    def _():
        qk_ref[...] = jnp.zeros_like(qk_ref)

    weights = [
        jnp.concatenate([qk_w_ref[k, n * depth : (n + 1) * depth] for n in range(2 * width // 128)], axis=1)
        for k in range(qk_w_ref.shape[0])
    ]
    qk_ref[...] += jnp.dot(
        states_ref[...], jnp.concatenate(weights, axis=0), preferred_element_type=F32
    )

    @pl.when(i == pl.num_programs(0) - 1)
    def _():
        slots = qk_ref.shape[0]
        ok = lax.broadcasted_iota(jnp.int32, (slots, slots), 1) < length_ref[0]
        for h in range(heads):
            cols = slice(h * HEAD, (h + 1) * HEAD)
            query = qk_ref[:, cols].astype(BF)
            key = qk_ref[:, width + h * HEAD : width + (h + 1) * HEAD].astype(BF)
            scores = lax.dot_general(
                query, key, (((1,), (1,)), ((), ())), preferred_element_type=F32
            )
            scores = jnp.where(ok, scores, -jnp.inf)
            expo = jnp.exp(scores - jnp.max(scores, axis=-1, keepdims=True))
            total = jnp.sum(expo, axis=-1, keepdims=True)
            mixed = jnp.dot(expo.astype(BF), v_ref[:, cols], preferred_element_type=F32)
            out_ref[:, cols] = (mixed / total).astype(BF)


def encoder(length, states, gathered, v):
    slots, width = v.shape
    pieces = gathered.shape[0]
    shard = states.shape[1] // pieces
    at_once = 8
    return pl.pallas_call(
        functools.partial(encoder_kernel, width // HEAD),
        grid=(pieces // at_once,),
        in_specs=[
            pl.BlockSpec(memory_space=pltpu.SMEM),
            pl.BlockSpec((slots, at_once * shard), lambda i: (0, i)),
            pl.BlockSpec(
                (pl.Element(at_once), pl.Element(2 * width // 128 * shard), pl.Element(128)),
                lambda i: (i * at_once, 0, 0),
            ),
            pl.BlockSpec(v.shape, lambda i: (0, 0)),
        ],
        out_specs=pl.BlockSpec(v.shape, lambda i: (0, 0)),
        out_shape=jax.ShapeDtypeStruct(v.shape, BF),
        scratch_shapes=[pltpu.VMEM((slots, 2 * width), F32)],
        compiler_params=pltpu.CompilerParams(vmem_limit_bytes=BIG),
        cost_estimate=pl.CostEstimate(
            flops=2 * slots * 2 * width * pieces * shard,
            bytes_accessed=pieces * 2 * shard * (slots + 2 * width),
            transcendentals=slots * slots * width // HEAD,
        ),
    )(length, states, gathered, v)


def context_kernel(mixed_ref, out_w_ref, mine_ref, weights_ref, out_ref, embedded_ref):
    blocks = embedded_ref.shape[0]

    @pl.when(pl.program_id(0) == 0)
    def _():
        for n in range(blocks):
            attn = 0
            for j in range(mixed_ref.shape[0]):
                attn += jnp.dot(
                    mixed_ref[j],
                    out_w_ref[j // 2 * NZ + 2 * n + j % 2],
                    preferred_element_type=F32,
                )
            mine = mine_ref[:, n * 128 : (n + 1) * 128].astype(F32)
            embedded_ref[n] = (mine + attn).astype(BF)

    for k in range(weights_ref.shape[0]):
        total = 0
        for n in range(blocks):
            total += lax.dot_general(
                weights_ref[k, n * PADDED : (n + 1) * PADDED],
                embedded_ref[n],
                (((1,), (1,)), ((), ())),
                preferred_element_type=F32,
            )
        out_ref[k] = total.astype(BF)


def embed_context(mixed, w_out, mine, gathered, row):
    slots, share = mine.shape
    blocks = share // 128
    pieces = gathered.shape[0]
    at_once = 8
    return pl.pallas_call(
        context_kernel,
        grid=(pieces // at_once,),
        in_specs=[
            pl.BlockSpec(mixed.shape, lambda i: (0, 0, 0)),
            pl.BlockSpec(w_out.shape, lambda i: (0, 0, 0)),
            pl.BlockSpec(mine.shape, lambda i: (0, 0)),
            pl.BlockSpec(
                (pl.Element(at_once), pl.Element(blocks * PADDED), pl.Element(128)),
                lambda i: (i * at_once, row, 0),
            ),
        ],
        out_specs=pl.BlockSpec((at_once, PADDED, slots), lambda i: (i, 0, 0)),
        out_shape=jax.ShapeDtypeStruct((pieces, PADDED, slots), BF),
        scratch_shapes=[pltpu.VMEM((blocks, slots, 128), BF)],
        compiler_params=pltpu.CompilerParams(vmem_limit_bytes=BIG),
        cost_estimate=pl.CostEstimate(
            flops=2 * pieces * PADDED * share * slots + 2 * slots * share * NX * NC * mixed.shape[2],
            bytes_accessed=pieces * PADDED * 2 * (share + slots),
            transcendentals=0,
        ),
    )(mixed, w_out, mine, gathered)


def image_kernel(image_ref, out_ref, stats_ref):
    local = out_ref.shape[1]
    stats_ref[...] = jnp.zeros_like(stats_ref)
    for h in range(local // HEAD):
        at = h * HEAD
        query = image_ref[:, at : at + HEAD]
        key = image_ref[:, local + at : local + at + HEAD]
        value = image_ref[:, 2 * local + at : 2 * local + at + HEAD]
        scores = lax.dot_general(query, key, (((1,), (1,)), ((), ())), preferred_element_type=F32)
        scores = scores * HEAD ** (-0.5)
        top = jnp.max(scores, axis=-1, keepdims=True)
        expo = jnp.exp(scores - top)
        out_ref[:, at : at + HEAD] = jnp.dot(expo.astype(BF), value, preferred_element_type=F32)
        stats_ref[:, 2 * h : 2 * h + 1] = top
        stats_ref[:, 2 * h + 1 : 2 * h + 2] = jnp.sum(expo, axis=-1, keepdims=True)


def attend_image(image):
    tokens, cols = image.shape
    vmem = pl.BlockSpec(memory_space=pltpu.VMEM)
    return pl.pallas_call(
        image_kernel,
        in_specs=[vmem],
        out_specs=[vmem, vmem],
        out_shape=[
            jax.ShapeDtypeStruct((tokens, cols // 3), F32),
            jax.ShapeDtypeStruct((tokens, 128), F32),
        ],
        compiler_params=pltpu.CompilerParams(vmem_limit_bytes=40 * 2**20),
        cost_estimate=pl.CostEstimate(
            flops=4 * tokens * tokens * cols // 3,
            bytes_accessed=tokens * cols * 6,
            transcendentals=tokens * tokens * cols // 3 // HEAD,
        ),
    )(image)


def joint_kernel(
    length_ref, context_ref, scale_ref, shift_ref, text_w_ref, query_ref, near_ref, stats_ref, out_ref
):
    pieces, rows, slots = context_ref.shape
    local = out_ref.shape[1]
    real = lax.broadcasted_iota(jnp.int32, (rows, slots), 0) < PIECE
    total = jnp.zeros((rows, slots), F32)
    for k in range(pieces):
        total += context_ref[k].astype(F32)
    mean = jnp.sum(total, axis=0, keepdims=True) / WIDTH
    square = jnp.zeros((rows, slots), F32)
    for k in range(pieces):
        centered = context_ref[k].astype(F32) - mean
        square += centered * centered
    square = jnp.where(real, square, 0.0)
    factor = lax.rsqrt(jnp.sum(square, axis=0, keepdims=True) / WIDTH + EPS)
    text = jnp.zeros((2 * local, slots), F32)
    for k in range(pieces):
        scale = 1.0 + jnp.concatenate([scale_ref[k]] * (slots // 128), axis=1)
        move = jnp.concatenate([shift_ref[k]] * (slots // 128), axis=1)
        modulated = (context_ref[k].astype(F32) - mean) * factor * scale + move
        modulated = jnp.where(real, modulated, 0.0).astype(BF)
        text += lax.dot_general(
            text_w_ref[k], modulated, (((0,), (0,)), ((), ())), preferred_element_type=F32
        )
    text = text.astype(BF)
    tokens = query_ref.shape[0]
    ok = lax.broadcasted_iota(jnp.int32, (tokens, slots), 1) < length_ref[0]
    for h in range(local // HEAD):
        at = h * HEAD
        query = query_ref[:, at : at + HEAD]
        far = jnp.dot(query, text[at : at + HEAD], preferred_element_type=F32) * HEAD ** (-0.5)
        far = jnp.where(ok, far, -jnp.inf)
        near_top = stats_ref[:, 2 * h : 2 * h + 1]
        top = jnp.maximum(near_top, jnp.max(far, axis=-1, keepdims=True))
        less = jnp.exp(near_top - top)
        far = jnp.exp(far - top)
        sums = stats_ref[:, 2 * h + 1 : 2 * h + 2] * less + jnp.sum(far, axis=-1, keepdims=True)
        result = near_ref[:, at : at + HEAD] * less
        result += lax.dot_general(
            far.astype(BF),
            text[local + at : local + at + HEAD],
            (((1,), (1,)), ((), ())),
            preferred_element_type=F32,
        )
        out_ref[:, at : at + HEAD] = (result / sums).astype(BF)


def joint(length, context, scale, move, text_w, query, near, stats):
    pieces, rows, slots = context.shape
    tokens, local = query.shape
    vmem = pl.BlockSpec(memory_space=pltpu.VMEM)
    return pl.pallas_call(
        joint_kernel,
        in_specs=[pl.BlockSpec(memory_space=pltpu.SMEM)] + [vmem] * 7,
        out_specs=vmem,
        out_shape=jax.ShapeDtypeStruct((tokens, local), BF),
        compiler_params=pltpu.CompilerParams(vmem_limit_bytes=40 * 2**20),
        cost_estimate=pl.CostEstimate(
            flops=4 * pieces * rows * local * slots + 4 * tokens * slots * local,
            bytes_accessed=pieces * rows * 2 * (slots + 2 * local),
            transcendentals=tokens * slots * local // HEAD,
        ),
    )(length, context, scale, move, text_w, query, near, stats)


def tensor_exchange(array):
    return lax.all_to_all(array, TENSOR, 0, 0, tiled=True)


def take(array, index, axis=0):
    return lax.dynamic_index_in_dim(array, index, axis, keepdims=False)


def other_core(array):
    return shift(array, "c", NC, 1)


def reduce_tensor(parts):
    x, c = lax.axis_index("x"), lax.axis_index("c")
    parts = parts.reshape((NX, NC) + parts.shape[1:])
    received = other_core(take(parts, 1 - c, 1))
    chip = (take(parts, c, 1).astype(F32) + received.astype(F32)).astype(parts.dtype)
    near = [shift(take(chip, (x + d) % NX), "x", NX, d) for d in (1, -1)]
    far = take(chip, (x + 2) % NX)
    half = far.shape[0] // 2
    far = [shift(far[:half], "x", NX, 2), shift(far[half:], "x", NX, -2)]
    far = jnp.concatenate(far, axis=0)
    total = take(chip, x).astype(F32) + near[0].astype(F32)
    return total + near[1].astype(F32) + far.astype(F32)


def gather_tensor(block):
    x, c = lax.axis_index("x"), lax.axis_index("c")
    line = jnp.zeros((NX,) + block.shape, block.dtype)
    pieces = [(0, block)] + [(-d, shift(block, "x", NX, d)) for d in (1, -1, 2)]
    for step, piece in pieces:
        line = lax.dynamic_update_slice_in_dim(line, piece[None], (x + step) % NX, 0)
    other = other_core(line)
    low, high = jnp.where(c == 0, line, other), jnp.where(c == 0, other, line)
    return jnp.stack([low, high], axis=1)


def per_device(
    text_states,
    prompt_lengths,
    attn_gain,
    query_w,
    key_w,
    value_w,
    out_w,
    context_w,
    mod_scale,
    mod_shift,
    text_key_w,
    text_value_w,
    image_query,
    image_key,
    image_value,
):
    slots, enc = text_states.shape[1:]
    ndev = NX * NC
    pieces = NY * NZ
    me = lax.axis_index("x") * NC + lax.axis_index("c")
    width = query_w.shape[1]
    shard = query_w.shape[0]
    share = enc // ndev
    moved = columns_to_devices(out_w)
    packed, text_w = pack(query_w, key_w, context_w, text_key_w, text_value_w)
    context_row = 2 * width // 128 * shard
    gathered = lax.all_gather(packed, DP, axis=0)
    moved = jnp.concatenate([moved[:shard], moved[shard:]], axis=1)
    block = gather_over_y(jnp.concatenate([value_w, moved], axis=0))
    later = (text_states, image_query, image_key, image_value, text_w)
    block, *later = lax.optimization_barrier((block, *later))
    text_states, image_query, image_key, image_value, text_w = later
    ring = ring_over_z(block)
    text_block = gather_over_y(text_w)
    *_, (step, last) = ring
    last, text_block = lax.optimization_barrier((last, text_block))
    ring[-1] = (step, last)
    text_w = place_z(ring_over_z(text_block), lambda piece: piece)
    text_w = text_w.reshape(pieces, PADDED, text_w.shape[-1])

    flat = text_states[0].astype(F32)
    scale = lax.rsqrt(jnp.mean(flat * flat, axis=-1, keepdims=True) + EPS)
    normed = (flat * scale * attn_gain).astype(BF)

    nheads = image_query.shape[-1] // HEAD // ndev
    local = nheads * HEAD
    tokens = image_query.shape[1]
    image = jnp.concatenate(
        [
            jnp.swapaxes(part[0].reshape(tokens, ndev, local), 0, 1)
            for part in (image_query, image_key, image_value)
        ],
        axis=-1,
    )
    image = tensor_exchange(image).reshape(ndev * tokens, 3 * local)

    v_all = place_z(ring, lambda piece: piece[:, :shard]).reshape(enc, width)
    w_out = place_z(
        ring, lambda piece: jnp.concatenate([piece[:, shard:, :128], piece[:, shard:, 128:]], axis=1)
    ).reshape(pieces, 2 * shard, shard)
    enc_v = jnp.dot(normed, v_all, preferred_element_type=F32).astype(BF)
    near, stats = attend_image(image)
    query = image[:, :local]

    def spaced(row):
        row = jnp.pad(row.reshape(pieces, PIECE), ((0, 0), (0, PADDED - PIECE)))
        return jnp.broadcast_to(row[:, :, None], (pieces, PADDED, 128))

    scale, move = spaced(mod_scale), spaced(mod_shift)
    mine = lax.dynamic_slice_in_dim(text_states[0], me * share, share, 1)
    ready = lax.optimization_barrier((enc_v, query, near, stats, scale, move, mine))
    enc_v, query, near, stats, scale, move, mine = ready

    mixed = encoder(prompt_lengths, normed, gathered, enc_v)
    mixed = gather_tensor(mixed).reshape(ndev, slots, width)
    context_part = embed_context(mixed, w_out, mine, gathered, context_row)
    context = reduce_tensor(context_part.reshape(ndev, pieces // ndev * PADDED, slots))
    context = gather_tensor(context.astype(BF)).reshape(pieces, PADDED, slots)
    result = joint(prompt_lengths, context, scale, move, text_w, query, near, stats)
    result = tensor_exchange(result.reshape(ndev, tokens, local))
    return jnp.swapaxes(result, 0, 1).reshape(1, tokens, ndev * local)


def solution(mesh):
    fine = Mesh(mesh.devices.reshape(NY, NZ, NX, NC), DP + TENSOR)
    in_specs = (
        P(DP, None, None),
        P(DP),
        P(),
        P(DP, TENSOR),
        P(DP, TENSOR),
        P(DP, TENSOR),
        P(TENSOR, DP),
        P(TENSOR, DP),
        P(DP, None),
        P(DP, None),
        P(DP, TENSOR),
        P(DP, TENSOR),
        P(DP, TENSOR, None),
        P(DP, TENSOR, None),
        P(DP, TENSOR, None),
    )
    out_specs = P(DP, TENSOR, None)
    return jax.shard_map(
        per_device, mesh=fine, in_specs=in_specs, out_specs=out_specs, check_vma=False
    )
```

```python
import functools

import jax
import jax.numpy as jnp
from jax import lax
from jax.experimental import pallas as pl
from jax.experimental.pallas import tpu as pltpu
from jax.sharding import Mesh
from jax.sharding import PartitionSpec as P

HEAD = 64
EPS = 1e-06
NY, NZ, NX, NC = 4, 8, 4, 2
DP = ("y", "z")
TENSOR = ("x", "c")
WIDTH = 2432
PIECE = 76
PADDED = 80
BF = jnp.bfloat16
F32 = jnp.float32
BIG = 56 * 2**20


def shift(array, axis, size, step):
    return lax.ppermute(array, axis, [(i, (i + step) % size) for i in range(size)])


def gather_over_y(shard):
    half = shard.shape[0] // 2
    y = lax.axis_index("y")
    up, down = shift(shard, "y", NY, 1), shift(shard, "y", NY, -1)
    far = [shift(up[:half], "y", NY, 1), shift(down[half:], "y", NY, -1)]
    far = jnp.concatenate(far, axis=0)
    block = jnp.zeros((NY,) + shard.shape, shard.dtype)
    for step, piece in ((0, shard), (-1, up), (1, down), (2, far)):
        block = lax.dynamic_update_slice_in_dim(block, piece[None], (y + step) % NY, 0)
    return block


def gather_over_z(shard, later):
    z = lax.axis_index("z")
    forward, backward = shift(shard, "z", NZ, 1), shift(shard, "z", NZ, -1)
    forward, backward, *later = lax.optimization_barrier((forward, backward, *later))
    found = [(0, shard), (-1, forward), (1, backward)]
    for step in (2, 3, 4):
        forward = shift(forward, "z", NZ, 1)
        found.append((-step, forward))
        if step < 4:
            backward = shift(backward, "z", NZ, -1)
            found.append((step, backward))
    line = jnp.zeros((NZ,) + shard.shape, shard.dtype)
    for step, piece in found:
        line = lax.dynamic_update_slice_in_dim(line, piece[None], (z + step) % NZ, 0)
    return line, later


def share_y(block):
    return lax.all_to_all(
        jnp.broadcast_to(block[None], (NY,) + block.shape), "y", 0, 0, tiled=True
    )


def ring_over_z(block):
    def z_pair(ahead, behind):
        return shift(ahead, "z", NZ, 1), shift(behind, "z", NZ, -1)

    s1, t1 = z_pair(block, block)
    s2, t2 = z_pair(s1, t1)
    s3, t3 = z_pair(s2, t2)
    s4 = shift(s3[: NY // 2], "z", NZ, 1)
    t4 = shift(t3[NY // 2 :], "z", NZ, -1)
    last = jnp.concatenate([s4, t4], axis=0)
    return [(0, block), (-1, s1), (1, t1), (-2, s2), (2, t2), (-3, s3), (3, t3), (4, last)]


def place_z(ring, split):
    z = lax.axis_index("z")
    pieces = [(step, split(block)) for step, block in ring]
    whole = jnp.zeros((NY, NZ) + pieces[0][1].shape[1:], pieces[0][1].dtype)
    for step, piece in pieces:
        whole = lax.dynamic_update_slice_in_dim(whole, piece[:, None], (z + step) % NZ, 1)
    return whole


def columns_to_devices(out_w):
    pairs = []
    for y in range(NY):
        for z in range(NZ):
            for x in range(NX):
                for c in range(NC):
                    source = ((x * NZ + 4 * c + z // 2) * NX + y) * NC + z % 2
                    pairs.append((source, ((y * NZ + z) * NX + x) * NC + c))
    return lax.ppermute(out_w, DP + TENSOR, pairs)


def pack_kernel(query_ref, key_ref, context_ref, key_w_ref, value_w_ref, out_ref, spare_ref, flat_ref):
    shard = query_ref.shape[0]
    row = 0
    for ref in (query_ref, key_ref):
        for n in range(0, ref.shape[1], 128):
            out_ref[row : row + shard] = ref[:, n : n + 128]
            row += shard
    spare_ref[...] = jnp.zeros_like(spare_ref)
    spare_ref[:, :PIECE] = context_ref[...].astype(F32)
    for n in range(0, spare_ref.shape[0], 128):
        turned = spare_ref[n : n + 128].T
        out_ref[row : row + PADDED] = turned[:PADDED].astype(BF)
        row += PADDED
    flat_ref[...] = jnp.zeros_like(flat_ref)
    local = key_w_ref.shape[1]
    flat_ref[:PIECE, :local] = key_w_ref[...].astype(F32)
    flat_ref[:PIECE, local:] = value_w_ref[...].astype(F32)
    for n in range(0, 2 * local, 128):
        out_ref[row : row + PADDED] = flat_ref[:, n : n + 128].astype(BF)
        row += PADDED


def pack(query_w, key_w, context_w, text_key_w, text_value_w):
    cols = 2 * text_key_w.shape[1]
    rows = 2 * query_w.shape[0] * query_w.shape[1] // 128
    rows += (context_w.shape[0] + cols) // 128 * PADDED
    vmem = pl.BlockSpec(memory_space=pltpu.VMEM)
    return pl.pallas_call(
        pack_kernel,
        in_specs=[vmem] * 5,
        out_specs=vmem,
        out_shape=jax.ShapeDtypeStruct((rows, 128), BF),
        scratch_shapes=[
            pltpu.VMEM((context_w.shape[0], 128), F32),
            pltpu.VMEM((PADDED, cols), F32),
        ],
        compiler_params=pltpu.CompilerParams(vmem_limit_bytes=40 * 2**20),
    )(query_w, key_w, context_w, text_key_w, text_value_w)


def encoder_kernel(heads, length_ref, states_ref, qk_w_ref, v_ref, out_ref, qk_ref):
    i = pl.program_id(0)
    width = heads * HEAD
    depth = qk_w_ref.shape[1] * 128 // (2 * width)

    @pl.when(i == 0)
    def _():
        qk_ref[...] = jnp.zeros_like(qk_ref)

    weights = [
        jnp.concatenate([qk_w_ref[k, n * depth : (n + 1) * depth] for n in range(2 * width // 128)], axis=1)
        for k in range(qk_w_ref.shape[0])
    ]
    qk_ref[...] += jnp.dot(
        states_ref[...], jnp.concatenate(weights, axis=0), preferred_element_type=F32
    )

    @pl.when(i == pl.num_programs(0) - 1)
    def _():
        slots = qk_ref.shape[0]
        ok = lax.broadcasted_iota(jnp.int32, (slots, slots), 1) < length_ref[0]
        for h in range(heads):
            cols = slice(h * HEAD, (h + 1) * HEAD)
            query = qk_ref[:, cols].astype(BF)
            key = qk_ref[:, width + h * HEAD : width + (h + 1) * HEAD].astype(BF)
            scores = lax.dot_general(
                query, key, (((1,), (1,)), ((), ())), preferred_element_type=F32
            )
            scores = jnp.where(ok, scores, -jnp.inf)
            expo = jnp.exp(scores - jnp.max(scores, axis=-1, keepdims=True))
            total = jnp.sum(expo, axis=-1, keepdims=True)
            mixed = jnp.dot(expo.astype(BF), v_ref[:, cols], preferred_element_type=F32)
            out_ref[:, cols] = (mixed / total).astype(BF)


def encoder(length, states, gathered, v):
    slots, width = v.shape
    pieces = gathered.shape[0]
    shard = states.shape[1] // pieces
    at_once = 8
    return pl.pallas_call(
        functools.partial(encoder_kernel, width // HEAD),
        grid=(pieces // at_once,),
        in_specs=[
            pl.BlockSpec(memory_space=pltpu.SMEM),
            pl.BlockSpec((slots, at_once * shard), lambda i: (0, i)),
            pl.BlockSpec(
                (pl.Element(at_once), pl.Element(2 * width // 128 * shard), pl.Element(128)),
                lambda i: (i * at_once, 0, 0),
            ),
            pl.BlockSpec(v.shape, lambda i: (0, 0)),
        ],
        out_specs=pl.BlockSpec(v.shape, lambda i: (0, 0)),
        out_shape=jax.ShapeDtypeStruct(v.shape, BF),
        scratch_shapes=[pltpu.VMEM((slots, 2 * width), F32)],
        compiler_params=pltpu.CompilerParams(vmem_limit_bytes=BIG),
        cost_estimate=pl.CostEstimate(
            flops=2 * slots * 2 * width * pieces * shard,
            bytes_accessed=pieces * 2 * shard * (slots + 2 * width),
            transcendentals=slots * slots * width // HEAD,
        ),
    )(length, states, gathered, v)


def embed_kernel(rows_ref, near_ref, other_ref, out_w_ref, mine_ref, out_ref):
    for n in range(mine_ref.shape[1] // 128):
        attn = 0
        for r in range(NX):
            for core, ref in ((0, near_ref), (1, other_ref)):
                weights = out_w_ref[rows_ref[r, core] // 2 * NZ + 2 * n + rows_ref[r, core] % 2]
                attn += jnp.dot(ref[r], weights, preferred_element_type=F32)
        cols = slice(n * 128, (n + 1) * 128)
        out_ref[cols] = (mine_ref[:, cols].astype(F32) + attn).T.astype(BF)


def embed(rows, near, other, w_out, mine):
    slots, share = mine.shape
    vmem = pl.BlockSpec(memory_space=pltpu.VMEM)
    return pl.pallas_call(
        embed_kernel,
        in_specs=[pl.BlockSpec(memory_space=pltpu.SMEM)] + [vmem] * 4,
        out_specs=vmem,
        out_shape=jax.ShapeDtypeStruct((share, slots), BF),
        compiler_params=pltpu.CompilerParams(vmem_limit_bytes=40 * 2**20),
        cost_estimate=pl.CostEstimate(
            flops=4 * slots * share * NX * near.shape[2],
            bytes_accessed=w_out.size * 2 + near.size * 4,
            transcendentals=0,
        ),
    )(rows, near, other, w_out, mine)


def context_kernel(order_ref, embedded_ref, weights_ref, out_ref):
    del order_ref
    for k in range(weights_ref.shape[0]):
        weights = [
            weights_ref[k, n : n + PADDED] for n in range(0, weights_ref.shape[1], PADDED)
        ]
        out_ref[0, k] = jnp.dot(
            jnp.concatenate(weights, axis=1), embedded_ref[...], preferred_element_type=F32
        ).astype(BF)


def embed_context(order, embedded, gathered, row):
    share, slots = embedded.shape
    each = gathered.shape[0] // (NX * NC)
    out = (each, PADDED, slots)
    return pl.pallas_call(
        context_kernel,
        grid_spec=pltpu.PrefetchScalarGridSpec(
            num_scalar_prefetch=1,
            grid=(NX,),
            in_specs=[
                pl.BlockSpec(embedded.shape, lambda i, order: (0, 0)),
                pl.BlockSpec(
                    (pl.Element(each), pl.Element(share // 128 * PADDED), pl.Element(128)),
                    lambda i, order: (order[i] * each, row, 0),
                ),
            ],
            out_specs=pl.BlockSpec((1,) + out, lambda i, order: (i, 0, 0, 0)),
        ),
        out_shape=jax.ShapeDtypeStruct((NX,) + out, BF),
        compiler_params=pltpu.CompilerParams(vmem_limit_bytes=BIG),
        cost_estimate=pl.CostEstimate(
            flops=2 * NX * each * PADDED * share * slots,
            bytes_accessed=NX * each * PADDED * 2 * (share + slots),
            transcendentals=0,
        ),
    )(order, embedded, gathered)


def image_kernel(image_ref, out_ref, stats_ref):
    local = out_ref.shape[1]
    stats_ref[...] = jnp.zeros_like(stats_ref)
    for h in range(local // HEAD):
        at = h * HEAD
        query = image_ref[:, at : at + HEAD]
        key = image_ref[:, local + at : local + at + HEAD]
        value = image_ref[:, 2 * local + at : 2 * local + at + HEAD]
        scores = lax.dot_general(query, key, (((1,), (1,)), ((), ())), preferred_element_type=F32)
        scores = scores * HEAD ** (-0.5)
        top = jnp.max(scores, axis=-1, keepdims=True)
        expo = jnp.exp(scores - top)
        out_ref[:, at : at + HEAD] = jnp.dot(expo.astype(BF), value, preferred_element_type=F32)
        stats_ref[:, 2 * h : 2 * h + 1] = top
        stats_ref[:, 2 * h + 1 : 2 * h + 2] = jnp.sum(expo, axis=-1, keepdims=True)


def attend_image(image):
    tokens, cols = image.shape
    vmem = pl.BlockSpec(memory_space=pltpu.VMEM)
    return pl.pallas_call(
        image_kernel,
        in_specs=[vmem],
        out_specs=[vmem, vmem],
        out_shape=[
            jax.ShapeDtypeStruct((tokens, cols // 3), F32),
            jax.ShapeDtypeStruct((tokens, 128), F32),
        ],
        compiler_params=pltpu.CompilerParams(vmem_limit_bytes=40 * 2**20),
        cost_estimate=pl.CostEstimate(
            flops=4 * tokens * tokens * cols // 3,
            bytes_accessed=tokens * cols * 6,
            transcendentals=tokens * tokens * cols // 3 // HEAD,
        ),
    )(image)


def joint_kernel(
    row,
    length_ref,
    order_ref,
    near_ref,
    other_ref,
    scale_ref,
    shift_ref,
    gathered_ref,
    query_ref,
    image_ref,
    stats_ref,
    out_ref,
    text_ref,
    sem,
):
    _, each, rows, slots = near_ref.shape
    local = out_ref.shape[1]
    cols = text_ref.shape[1] // rows
    copy = pltpu.make_async_copy(
        gathered_ref.at[:, pl.ds(row, cols * rows)], text_ref, sem.at[0]
    )
    copy.start()
    real = lax.broadcasted_iota(jnp.int32, (rows, slots), 0) < PIECE
    parts = [(r, core, k) for r in range(NX) for core in range(NC) for k in range(each)]

    def context(part):
        r, core, k = part
        return (near_ref, other_ref)[core][r, k].astype(F32)

    total = jnp.zeros((rows, slots), F32)
    for part in parts:
        total += context(part)
    mean = jnp.sum(total, axis=0, keepdims=True) / WIDTH
    square = jnp.zeros((rows, slots), F32)
    for part in parts:
        centered = context(part) - mean
        square += centered * centered
    square = jnp.where(real, square, 0.0)
    factor = lax.rsqrt(jnp.sum(square, axis=0, keepdims=True) / WIDTH + EPS)
    copy.wait()
    text = jnp.zeros((2 * local, slots), F32)
    for part in parts:
        r, core, k = part
        at = order_ref[r, core] * each + k
        scale = 1.0 + jnp.concatenate([scale_ref[at]] * (slots // 128), axis=1)
        move = jnp.concatenate([shift_ref[at]] * (slots // 128), axis=1)
        modulated = (context(part) - mean) * factor * scale + move
        modulated = jnp.where(real, modulated, 0.0).astype(BF)
        weights = [text_ref[at, n * rows : (n + 1) * rows] for n in range(cols)]
        text += lax.dot_general(
            jnp.concatenate(weights, axis=1),
            modulated,
            (((0,), (0,)), ((), ())),
            preferred_element_type=F32,
        )
    text = text.astype(BF)
    tokens = query_ref.shape[0]
    ok = lax.broadcasted_iota(jnp.int32, (tokens, slots), 1) < length_ref[0]
    for h in range(local // HEAD):
        at = h * HEAD
        query = query_ref[:, at : at + HEAD]
        far = jnp.dot(query, text[at : at + HEAD], preferred_element_type=F32) * HEAD ** (-0.5)
        far = jnp.where(ok, far, -jnp.inf)
        near_top = stats_ref[:, 2 * h : 2 * h + 1]
        top = jnp.maximum(near_top, jnp.max(far, axis=-1, keepdims=True))
        less = jnp.exp(near_top - top)
        far = jnp.exp(far - top)
        sums = stats_ref[:, 2 * h + 1 : 2 * h + 2] * less + jnp.sum(far, axis=-1, keepdims=True)
        result = image_ref[:, at : at + HEAD] * less
        result += lax.dot_general(
            far.astype(BF),
            text[local + at : local + at + HEAD],
            (((1,), (1,)), ((), ())),
            preferred_element_type=F32,
        )
        out_ref[:, at : at + HEAD] = (result / sums).astype(BF)


def joint(length, order, near, other, scale, move, gathered, row, query, image, stats):
    _, each, rows, slots = near.shape
    tokens, local = query.shape
    pieces = gathered.shape[0]
    text_rows = gathered.shape[1] - row
    vmem = pl.BlockSpec(memory_space=pltpu.VMEM)
    smem = pl.BlockSpec(memory_space=pltpu.SMEM)
    return pl.pallas_call(
        functools.partial(joint_kernel, row),
        in_specs=[smem] * 2 + [vmem] * 4 + [pl.BlockSpec(memory_space=pl.ANY)] + [vmem] * 3,
        out_specs=vmem,
        out_shape=jax.ShapeDtypeStruct((tokens, local), BF),
        scratch_shapes=[
            pltpu.VMEM((pieces, text_rows, 128), BF),
            pltpu.SemaphoreType.DMA((1,)),
        ],
        compiler_params=pltpu.CompilerParams(vmem_limit_bytes=48 * 2**20),
        cost_estimate=pl.CostEstimate(
            flops=4 * pieces * rows * local * slots + 4 * tokens * slots * local,
            bytes_accessed=pieces * rows * 2 * (slots + 2 * local),
            transcendentals=tokens * slots * local // HEAD,
        ),
    )(length, order, near, other, scale, move, gathered, query, image, stats)


def tensor_exchange(array):
    return lax.all_to_all(array, TENSOR, 0, 0, tiled=True)


def take(array, index, axis=0):
    return lax.dynamic_index_in_dim(array, index, axis, keepdims=False)


def other_core(array):
    return shift(array, "c", NC, 1)


FROM = (0, -1, 1, 2)


def reduce_tensor(keep, give):
    chip = (keep.astype(F32) + other_core(give).astype(F32)).astype(keep.dtype)
    half = chip.shape[1] // 2
    far = [shift(chip[3, :half], "x", NX, 2), shift(chip[3, half:], "x", NX, -2)]
    near = [shift(chip[1], "x", NX, 1), shift(chip[2], "x", NX, -1)]
    total = chip[0].astype(F32) + near[0].astype(F32) + near[1].astype(F32)
    return total + jnp.concatenate(far, axis=0).astype(F32)


def gather_tensor(block):
    far = shift(block, "x", NX, 2)
    line = jnp.stack([block, shift(block, "x", NX, 1), shift(block, "x", NX, -1), far])
    return line, other_core(line)


def per_device(
    text_states,
    prompt_lengths,
    attn_gain,
    query_w,
    key_w,
    value_w,
    out_w,
    context_w,
    mod_scale,
    mod_shift,
    text_key_w,
    text_value_w,
    image_query,
    image_key,
    image_value,
):
    slots, enc = text_states.shape[1:]
    ndev = NX * NC
    pieces = NY * NZ
    me = lax.axis_index("x") * NC + lax.axis_index("c")
    width = query_w.shape[1]
    shard = query_w.shape[0]
    share = enc // ndev
    moved = columns_to_devices(out_w)
    packed = pack(query_w, key_w, context_w, text_key_w, text_value_w)
    context_row = 2 * width // 128 * shard
    text_row = context_row + share // 128 * PADDED
    gathered = lax.all_gather(packed, DP, axis=0)
    out_block = gather_over_y(moved)
    line, images = gather_over_z(value_w, (image_query, image_key, image_value))
    image_query, image_key, image_value = images
    out_block, text_states = lax.optimization_barrier((out_block, text_states))

    flat = text_states[0].astype(F32)
    scale = lax.rsqrt(jnp.mean(flat * flat, axis=-1, keepdims=True) + EPS)
    normed = (flat * scale * attn_gain).astype(BF)

    nheads = image_query.shape[-1] // HEAD // ndev
    local = nheads * HEAD
    tokens = image_query.shape[1]
    image = jnp.concatenate(
        [
            jnp.swapaxes(part[0].reshape(tokens, ndev, local), 0, 1)
            for part in (image_query, image_key, image_value)
        ],
        axis=-1,
    )
    image = tensor_exchange(image).reshape(ndev * tokens, 3 * local)

    v_all = share_y(line).reshape(enc, width)
    w_out = place_z(ring_over_z(out_block), lambda piece: piece)
    w_out = w_out.reshape(pieces, 2 * shard, shard)
    enc_v = jnp.dot(normed, v_all, preferred_element_type=F32).astype(BF)
    near, stats = attend_image(image)
    query = image[:, :local]

    def spaced(row):
        row = jnp.pad(row.reshape(pieces, PIECE), ((0, 0), (0, PADDED - PIECE)))
        return jnp.broadcast_to(row[:, :, None], (pieces, PADDED, 128))

    scale, move = spaced(mod_scale), spaced(mod_shift)
    mine = lax.dynamic_slice_in_dim(text_states[0], me * share, share, 1)
    ready = lax.optimization_barrier((enc_v, query, near, stats, scale, move, mine))
    enc_v, query, near, stats, scale, move, mine = ready

    x, c = lax.axis_index("x"), lax.axis_index("c")
    chips = (x + jnp.array(FROM, jnp.int32)) % NX * NC
    order = jnp.stack([chips + c, chips + 1 - c], axis=1)
    targets = (x - jnp.array(FROM, jnp.int32)) % NX * NC
    mixed = encoder(prompt_lengths, normed, gathered, enc_v)
    near_mixed, other_mixed = gather_tensor(mixed)
    embedded = embed(order, near_mixed, other_mixed, w_out, mine)
    give = embed_context(targets + 1 - c, embedded, gathered, context_row)
    keep = embed_context(targets + c, embedded, gathered, context_row)
    context = reduce_tensor(keep, give).astype(BF)
    near_context, other_context = gather_tensor(context)
    result = joint(
        prompt_lengths,
        order,
        near_context,
        other_context,
        scale,
        move,
        gathered,
        text_row,
        query,
        near,
        stats,
    )
    result = tensor_exchange(result.reshape(ndev, tokens, local))
    return jnp.swapaxes(result, 0, 1).reshape(1, tokens, ndev * local)


def solution(mesh):
    fine = Mesh(mesh.devices.reshape(NY, NZ, NX, NC), DP + TENSOR)
    in_specs = (
        P(DP, None, None),
        P(DP),
        P(),
        P(DP, TENSOR),
        P(DP, TENSOR),
        P(DP, TENSOR),
        P(TENSOR, DP),
        P(TENSOR, DP),
        P(DP, None),
        P(DP, None),
        P(DP, TENSOR),
        P(DP, TENSOR),
        P(DP, TENSOR, None),
        P(DP, TENSOR, None),
        P(DP, TENSOR, None),
    )
    out_specs = P(DP, TENSOR, None)
    return jax.shard_map(
        per_device, mesh=fine, in_specs=in_specs, out_specs=out_specs, check_vma=False
    )
```

```python
import functools

import jax
import jax.numpy as jnp
from jax import lax
from jax.experimental import pallas as pl
from jax.experimental.pallas import tpu as pltpu
from jax.sharding import Mesh
from jax.sharding import PartitionSpec as P

HEAD = 64
EPS = 1e-06
NY, NZ, NX, NC = 4, 8, 4, 2
DP = ("y", "z")
TENSOR = ("x", "c")
WIDTH = 2432
PIECE = 76
PADDED = 80
BF = jnp.bfloat16
F32 = jnp.float32
BIG = 56 * 2**20


def shift(array, axis, size, step):
    return lax.ppermute(array, axis, [(i, (i + step) % size) for i in range(size)])


def gather_over_y(shard):
    half = shard.shape[0] // 2
    y = lax.axis_index("y")
    up, down = shift(shard, "y", NY, 1), shift(shard, "y", NY, -1)
    far = [shift(up[:half], "y", NY, 1), shift(down[half:], "y", NY, -1)]
    far = jnp.concatenate(far, axis=0)
    block = jnp.zeros((NY,) + shard.shape, shard.dtype)
    for step, piece in ((0, shard), (-1, up), (1, down), (2, far)):
        block = lax.dynamic_update_slice_in_dim(block, piece[None], (y + step) % NY, 0)
    return block


def gather_over_z(shard, later):
    z = lax.axis_index("z")
    forward, backward = shift(shard, "z", NZ, 1), shift(shard, "z", NZ, -1)
    forward, backward, *later = lax.optimization_barrier((forward, backward, *later))
    found = [(0, shard), (-1, forward), (1, backward)]
    for step in (2, 3, 4):
        forward = shift(forward, "z", NZ, 1)
        found.append((-step, forward))
        if step < 4:
            backward = shift(backward, "z", NZ, -1)
            found.append((step, backward))
    line = jnp.zeros((NZ,) + shard.shape, shard.dtype)
    for step, piece in found:
        line = lax.dynamic_update_slice_in_dim(line, piece[None], (z + step) % NZ, 0)
    return line, later


def share_y(block):
    return lax.all_to_all(
        jnp.broadcast_to(block[None], (NY,) + block.shape), "y", 0, 0, tiled=True
    )


def ring_over_z(block):
    def z_pair(ahead, behind):
        return shift(ahead, "z", NZ, 1), shift(behind, "z", NZ, -1)

    s1, t1 = z_pair(block, block)
    s2, t2 = z_pair(s1, t1)
    s3, t3 = z_pair(s2, t2)
    s4 = shift(s3[: NY // 2], "z", NZ, 1)
    t4 = shift(t3[NY // 2 :], "z", NZ, -1)
    last = jnp.concatenate([s4, t4], axis=0)
    return [(0, block), (-1, s1), (1, t1), (-2, s2), (2, t2), (-3, s3), (3, t3), (4, last)]


def place_z(ring, split):
    z = lax.axis_index("z")
    pieces = [(step, split(block)) for step, block in ring]
    whole = jnp.zeros((NY, NZ) + pieces[0][1].shape[1:], pieces[0][1].dtype)
    for step, piece in pieces:
        whole = lax.dynamic_update_slice_in_dim(whole, piece[:, None], (z + step) % NZ, 1)
    return whole


def columns_to_devices(out_w):
    pairs = []
    for y in range(NY):
        for z in range(NZ):
            for x in range(NX):
                for c in range(NC):
                    source = ((x * NZ + 4 * c + z // 2) * NX + y) * NC + z % 2
                    pairs.append((source, ((y * NZ + z) * NX + x) * NC + c))
    return lax.ppermute(out_w, DP + TENSOR, pairs)


def pack_kernel(context_ref, key_w_ref, value_w_ref, moved_ref, out_ref, spare_ref, flat_ref):
    row = 0
    spare_ref[...] = jnp.zeros_like(spare_ref)
    spare_ref[:, :PIECE] = context_ref[...].astype(F32)
    for n in range(0, spare_ref.shape[0], 128):
        turned = spare_ref[n : n + 128].T
        out_ref[row : row + PADDED] = turned[:PADDED].astype(BF)
        row += PADDED
    flat_ref[...] = jnp.zeros_like(flat_ref)
    local = key_w_ref.shape[1]
    flat_ref[:PIECE, :local] = key_w_ref[...].astype(F32)
    flat_ref[:PIECE, local:] = value_w_ref[...].astype(F32)
    for n in range(0, 2 * local, 128):
        out_ref[row : row + PADDED] = flat_ref[:, n : n + 128].astype(BF)
        row += PADDED
    out_ref[row:] = moved_ref[...]


def pack(context_w, text_key_w, text_value_w, moved):
    cols = 2 * text_key_w.shape[1]
    rows = (context_w.shape[0] + cols) // 128 * PADDED + moved.shape[0]
    vmem = pl.BlockSpec(memory_space=pltpu.VMEM)
    return pl.pallas_call(
        pack_kernel,
        in_specs=[vmem] * 4,
        out_specs=vmem,
        out_shape=jax.ShapeDtypeStruct((rows, 128), BF),
        scratch_shapes=[
            pltpu.VMEM((context_w.shape[0], 128), F32),
            pltpu.VMEM((PADDED, cols), F32),
        ],
        compiler_params=pltpu.CompilerParams(vmem_limit_bytes=40 * 2**20),
    )(context_w, text_key_w, text_value_w, moved)


def encoder_kernel(
    lengths_ref, order_ref, mine_ref, near_ref, other_ref, weights_ref, out_ref, theirs_ref, qkv_ref
):
    i = pl.program_id(0)
    slots, width = out_ref.shape
    some = slots // (NX * NC)

    @pl.when(i == 0)
    def _():
        qkv_ref[...] = jnp.zeros_like(qkv_ref)

    states = [mine_ref[...]] + [ref[r] for r in range(NX) for ref in (near_ref, other_ref)]
    qkv_ref[...] += jnp.dot(
        jnp.concatenate(states, axis=0), weights_ref[...], preferred_element_type=F32
    )

    @pl.when(i == pl.num_programs(0) - 1)
    def _():
        lane = lax.broadcasted_iota(jnp.int32, (slots, slots), 1)
        place = jnp.zeros((slots, slots), jnp.int32)
        for n in range(NX * NC):
            start = (order_ref[n // NC, n % NC] - n) * some
            place += jnp.where(lane // some == n, start, 0)
        for sample, ok in enumerate((lane < lengths_ref[0], lane + place < lengths_ref[1])):
            rows = slice(sample * slots, (sample + 1) * slots)
            results = []
            for h in range(width // HEAD):
                query, key, value = (
                    qkv_ref[rows, part * width + h * HEAD : part * width + (h + 1) * HEAD].astype(BF)
                    for part in range(3)
                )
                scores = lax.dot_general(
                    query, key, (((1,), (1,)), ((), ())), preferred_element_type=F32
                )
                scores = jnp.where(ok, scores, -jnp.inf)
                expo = jnp.exp(scores - jnp.max(scores, axis=-1, keepdims=True))
                total = jnp.sum(expo, axis=-1, keepdims=True)
                mixed = jnp.dot(expo.astype(BF), value, preferred_element_type=F32)
                results.append(mixed / total)
            mixed = jnp.concatenate(results, axis=1).astype(BF)
            if sample == 0:
                out_ref[...] = mixed
            else:
                for n in range(NX * NC):
                    at = pl.multiple_of(order_ref[n // NC, n % NC] * some, some)
                    theirs_ref[pl.ds(at, some)] = mixed[n * some : (n + 1) * some]


def encoder(lengths, order, mine, near, other, weights):
    slots, enc = mine.shape
    cols = weights.shape[1]
    steps = 4
    smem = pl.BlockSpec(memory_space=pltpu.SMEM)
    out = pl.BlockSpec((slots, cols // 3), lambda i: (0, 0))
    line = pl.BlockSpec(near.shape[:2] + (enc // steps,), lambda i: (0, 0, i))
    return pl.pallas_call(
        encoder_kernel,
        grid=(steps,),
        in_specs=[
            smem,
            smem,
            pl.BlockSpec((slots, enc // steps), lambda i: (0, i)),
            line,
            line,
            pl.BlockSpec((enc // steps, cols), lambda i: (i, 0)),
        ],
        out_specs=[out, out],
        out_shape=[jax.ShapeDtypeStruct((slots, cols // 3), BF)] * 2,
        scratch_shapes=[pltpu.VMEM((2 * slots, cols), F32)],
        compiler_params=pltpu.CompilerParams(vmem_limit_bytes=40 * 2**20),
        cost_estimate=pl.CostEstimate(
            flops=4 * slots * enc * cols,
            bytes_accessed=2 * enc * (2 * slots + cols),
            transcendentals=2 * slots * slots * cols // 3 // HEAD,
        ),
    )(lengths, order, mine, near, other, weights)


def embed_kernel(rows_ref, near_ref, other_ref, out_w_ref, mine_ref, out_ref):
    half = near_ref.shape[2] // 2
    for n in range(mine_ref.shape[1] // 128):
        attn = 0
        for r in range(NX):
            for core, ref in ((0, near_ref), (1, other_ref)):
                at = rows_ref[r, core] // 2 * NZ + 2 * n + rows_ref[r, core] % 2
                for part in range(2):
                    start = pl.multiple_of(rows_ref[NX, part] * half, half)
                    attn += jnp.dot(
                        ref[r, :, part * half : (part + 1) * half],
                        out_w_ref[at, pl.ds(start, half)],
                        preferred_element_type=F32,
                    )
        cols = slice(n * 128, (n + 1) * 128)
        out_ref[cols] = (mine_ref[:, cols].astype(F32) + attn).T.astype(BF)


def embed(rows, near, other, gathered, row, mine):
    slots, share = mine.shape
    width = near.shape[2]
    pieces = gathered.shape[0]

    def whole(array):
        return pl.BlockSpec(array.shape, lambda i: (0,) * array.ndim)

    return pl.pallas_call(
        embed_kernel,
        grid=(1,),
        in_specs=[
            pl.BlockSpec(memory_space=pltpu.SMEM),
            whole(near),
            whole(other),
            pl.BlockSpec(
                (pl.Element(pieces), pl.Element(width), pl.Element(128)), lambda i: (0, row, 0)
            ),
            whole(mine),
        ],
        out_specs=pl.BlockSpec((share, slots), lambda i: (0, 0)),
        out_shape=jax.ShapeDtypeStruct((share, slots), BF),
        compiler_params=pltpu.CompilerParams(vmem_limit_bytes=BIG),
        cost_estimate=pl.CostEstimate(
            flops=4 * slots * share * NX * width,
            bytes_accessed=pieces * width * 256 + near.size * 4,
            transcendentals=0,
        ),
    )(rows, near, other, gathered, mine)


def context_kernel(order_ref, embedded_ref, weights_ref, out_ref):
    del order_ref
    each, rows, _ = weights_ref.shape
    weights = [
        jnp.concatenate([weights_ref[k, n : n + PADDED] for n in range(0, rows, PADDED)], axis=1)
        for k in range(each)
    ]
    part = jnp.dot(
        jnp.concatenate(weights, axis=0), embedded_ref[...], preferred_element_type=F32
    ).astype(BF)
    for k in range(each):
        out_ref[0, k] = part[k * PADDED : (k + 1) * PADDED]


def embed_context(order, embedded, gathered, row):
    share, slots = embedded.shape
    each = gathered.shape[0] // (NX * NC)
    out = (each, PADDED, slots)
    return pl.pallas_call(
        context_kernel,
        grid_spec=pltpu.PrefetchScalarGridSpec(
            num_scalar_prefetch=1,
            grid=(NX,),
            in_specs=[
                pl.BlockSpec(embedded.shape, lambda i, order: (0, 0)),
                pl.BlockSpec(
                    (pl.Element(each), pl.Element(share // 128 * PADDED), pl.Element(128)),
                    lambda i, order: (order[i] * each, row, 0),
                ),
            ],
            out_specs=pl.BlockSpec((1,) + out, lambda i, order: (i, 0, 0, 0)),
        ),
        out_shape=jax.ShapeDtypeStruct((NX,) + out, BF),
        compiler_params=pltpu.CompilerParams(vmem_limit_bytes=BIG),
        cost_estimate=pl.CostEstimate(
            flops=2 * NX * each * PADDED * share * slots,
            bytes_accessed=NX * each * PADDED * 2 * (share + slots),
            transcendentals=0,
        ),
    )(order, embedded, gathered)


def image_kernel(image_ref, out_ref, stats_ref):
    local = out_ref.shape[1]
    stats_ref[...] = jnp.zeros_like(stats_ref)
    for h in range(local // HEAD):
        at = h * HEAD
        query = image_ref[:, at : at + HEAD]
        key = image_ref[:, local + at : local + at + HEAD]
        value = image_ref[:, 2 * local + at : 2 * local + at + HEAD]
        scores = lax.dot_general(query, key, (((1,), (1,)), ((), ())), preferred_element_type=F32)
        scores = scores * HEAD ** (-0.5)
        top = jnp.max(scores, axis=-1, keepdims=True)
        expo = jnp.exp(scores - top)
        out_ref[:, at : at + HEAD] = jnp.dot(expo.astype(BF), value, preferred_element_type=F32)
        stats_ref[:, 2 * h : 2 * h + 1] = top
        stats_ref[:, 2 * h + 1 : 2 * h + 2] = jnp.sum(expo, axis=-1, keepdims=True)


def attend_image(image):
    tokens, cols = image.shape
    vmem = pl.BlockSpec(memory_space=pltpu.VMEM)
    return pl.pallas_call(
        image_kernel,
        in_specs=[vmem],
        out_specs=[vmem, vmem],
        out_shape=[
            jax.ShapeDtypeStruct((tokens, cols // 3), F32),
            jax.ShapeDtypeStruct((tokens, 128), F32),
        ],
        compiler_params=pltpu.CompilerParams(vmem_limit_bytes=40 * 2**20),
        cost_estimate=pl.CostEstimate(
            flops=4 * tokens * tokens * cols // 3,
            bytes_accessed=tokens * cols * 6,
            transcendentals=tokens * tokens * cols // 3 // HEAD,
        ),
    )(image)


def joint_kernel(
    row,
    length_ref,
    order_ref,
    near_ref,
    other_ref,
    scale_ref,
    shift_ref,
    gathered_ref,
    query_ref,
    image_ref,
    stats_ref,
    out_ref,
    text_ref,
    states_ref,
    sem,
):
    _, each, rows, slots = near_ref.shape
    local = out_ref.shape[1]
    pieces = states_ref.shape[0]
    copies = [
        pltpu.make_async_copy(
            gathered_ref.at[:, pl.ds(row + n * rows, rows)],
            text_ref.at[:, :, pl.ds(n * 128, 128)],
            sem.at[n],
        )
        for n in range(2 * local // 128)
    ]
    for copy in copies:
        copy.start()
    real = lax.broadcasted_iota(jnp.int32, (rows, slots), 0) < PIECE
    parts = [(r, core, k) for r in range(NX) for core in range(NC) for k in range(each)]

    def context(part):
        r, core, k = part
        return (near_ref, other_ref)[core][r, k].astype(F32)

    total = jnp.zeros((rows, slots), F32)
    for part in parts:
        total += context(part)
    mean = jnp.sum(total, axis=0, keepdims=True) / WIDTH
    square = jnp.zeros((rows, slots), F32)
    for part in parts:
        centered = context(part) - mean
        square += centered * centered
    square = jnp.where(real, square, 0.0)
    factor = lax.rsqrt(jnp.sum(square, axis=0, keepdims=True) / WIDTH + EPS)
    for part in parts:
        r, core, k = part
        at = order_ref[r, core] * each + k
        scale = 1.0 + jnp.concatenate([scale_ref[at]] * (slots // 128), axis=1)
        move = jnp.concatenate([shift_ref[at]] * (slots // 128), axis=1)
        modulated = (context(part) - mean) * factor * scale + move
        states_ref[at] = jnp.where(real, modulated, 0.0).astype(BF)
    for copy in copies:
        copy.wait()
    text = lax.dot_general(
        text_ref[...].reshape(pieces * rows, 2 * local),
        states_ref[...].reshape(pieces * rows, slots),
        (((0,), (0,)), ((), ())),
        preferred_element_type=F32,
    )
    text = text.astype(BF)
    tokens = query_ref.shape[0]
    ok = lax.broadcasted_iota(jnp.int32, (tokens, slots), 1) < length_ref[0]
    for h in range(local // HEAD):
        at = h * HEAD
        query = query_ref[:, at : at + HEAD]
        far = jnp.dot(query, text[at : at + HEAD], preferred_element_type=F32) * HEAD ** (-0.5)
        far = jnp.where(ok, far, -jnp.inf)
        near_top = stats_ref[:, 2 * h : 2 * h + 1]
        top = jnp.maximum(near_top, jnp.max(far, axis=-1, keepdims=True))
        less = jnp.exp(near_top - top)
        far = jnp.exp(far - top)
        sums = stats_ref[:, 2 * h + 1 : 2 * h + 2] * less + jnp.sum(far, axis=-1, keepdims=True)
        result = image_ref[:, at : at + HEAD] * less
        result += lax.dot_general(
            far.astype(BF),
            text[local + at : local + at + HEAD],
            (((1,), (1,)), ((), ())),
            preferred_element_type=F32,
        )
        out_ref[:, at : at + HEAD] = (result / sums).astype(BF)


def joint(length, order, near, other, scale, move, gathered, row, query, image, stats):
    _, each, rows, slots = near.shape
    tokens, local = query.shape
    pieces = gathered.shape[0]
    vmem = pl.BlockSpec(memory_space=pltpu.VMEM)
    smem = pl.BlockSpec(memory_space=pltpu.SMEM)
    return pl.pallas_call(
        functools.partial(joint_kernel, row),
        in_specs=[smem] * 2 + [vmem] * 4 + [pl.BlockSpec(memory_space=pl.ANY)] + [vmem] * 3,
        out_specs=vmem,
        out_shape=jax.ShapeDtypeStruct((tokens, local), BF),
        scratch_shapes=[
            pltpu.VMEM((pieces, rows, 2 * local), BF),
            pltpu.VMEM((pieces, rows, slots), BF),
            pltpu.SemaphoreType.DMA((2 * local // 128,)),
        ],
        compiler_params=pltpu.CompilerParams(vmem_limit_bytes=48 * 2**20),
        cost_estimate=pl.CostEstimate(
            flops=4 * pieces * rows * local * slots + 4 * tokens * slots * local,
            bytes_accessed=pieces * rows * 2 * (slots + 2 * local),
            transcendentals=tokens * slots * local // HEAD,
        ),
    )(length, order, near, other, scale, move, gathered, query, image, stats)


def tensor_exchange(array):
    return lax.all_to_all(array, TENSOR, 0, 0, tiled=True)


def take(array, index, axis=0):
    return lax.dynamic_index_in_dim(array, index, axis, keepdims=False)


def other_core(array):
    return shift(array, "c", NC, 1)


FROM = (0, -1, 1, 2)


def reduce_tensor(keep, give):
    chip = (keep.astype(F32) + other_core(give).astype(F32)).astype(keep.dtype)
    half = chip.shape[1] // 2
    far = [shift(chip[3, :half], "x", NX, 2), shift(chip[3, half:], "x", NX, -2)]
    near = [shift(chip[1], "x", NX, 1), shift(chip[2], "x", NX, -1)]
    total = chip[0].astype(F32) + near[0].astype(F32) + near[1].astype(F32)
    return total + jnp.concatenate(far, axis=0).astype(F32)


def gather_tensor(block):
    far = shift(block, "x", NX, 2)
    line = jnp.stack([block, shift(block, "x", NX, 1), shift(block, "x", NX, -1), far])
    return line, other_core(line)


def per_device(
    text_states,
    prompt_lengths,
    attn_gain,
    query_w,
    key_w,
    value_w,
    out_w,
    context_w,
    mod_scale,
    mod_shift,
    text_key_w,
    text_value_w,
    image_query,
    image_key,
    image_value,
):
    slots, enc = text_states.shape[1:]
    ndev = NX * NC
    pieces = NY * NZ
    me = lax.axis_index("x") * NC + lax.axis_index("c")
    width = query_w.shape[1]
    half = width // 2
    share = enc // ndev
    y, x, c = (lax.axis_index(name) for name in "yxc")
    chips = (x + jnp.array(FROM, jnp.int32)) % NX * NC
    order = jnp.stack([chips + c, chips + 1 - c], axis=1)
    moved = columns_to_devices(out_w)
    packed = pack(context_w, text_key_w, text_value_w, moved)
    text_row = share // 128 * PADDED
    out_row = packed.shape[0] - out_w.shape[0]
    gathered = lax.all_gather(packed, DP, axis=0)

    odd = y % 2

    def heads(start):
        return jnp.concatenate(
            [lax.dynamic_slice_in_dim(w, start, half, 1) for w in (query_w, key_w, value_w)], axis=1
        )

    same, swapped = heads(odd * half), heads((1 - odd) * half)
    block = jnp.zeros((NY,) + same.shape, BF)
    found = [(0, same), (-1, shift(swapped, "y", NY, 1)), (1, shift(swapped, "y", NY, -1))]
    found.append((2, shift(same, "y", NY, 2)))
    for step, piece in found:
        block = lax.dynamic_update_slice_in_dim(block, piece[None], (y + step) % NY, 0)

    def partner(array):
        return lax.ppermute(array, "y", [(i, i ^ 1) for i in range(NY)])

    flat = text_states[0].astype(F32)
    scale = lax.rsqrt(jnp.mean(flat * flat, axis=-1, keepdims=True) + EPS)
    normed = (flat * scale * attn_gain).astype(BF)
    some = slots // ndev
    rows = partner(lax.dynamic_slice_in_dim(normed, me * some, some, 0))
    lengths = jnp.concatenate([prompt_lengths, partner(prompt_lengths)])
    images = (image_query, image_key, image_value)
    block, rows, *images = lax.optimization_barrier((block, rows, *images))
    image_query, image_key, image_value = images
    near_rows, other_rows = gather_tensor(rows)
    w_qkv = place_z(ring_over_z(block), lambda piece: piece).reshape(enc, 3 * half)

    nheads = image_query.shape[-1] // HEAD // ndev
    local = nheads * HEAD
    tokens = image_query.shape[1]
    image = jnp.concatenate(
        [
            jnp.swapaxes(part[0].reshape(tokens, ndev, local), 0, 1)
            for part in (image_query, image_key, image_value)
        ],
        axis=-1,
    )
    image = tensor_exchange(image).reshape(ndev * tokens, 3 * local)

    near, stats = attend_image(image)
    query = image[:, :local]

    def spaced(row):
        row = jnp.pad(row.reshape(pieces, PIECE), ((0, 0), (0, PADDED - PIECE)))
        return jnp.broadcast_to(row[:, :, None], (pieces, PADDED, 128))

    scale, move = spaced(mod_scale), spaced(mod_shift)
    mine = lax.dynamic_slice_in_dim(text_states[0], me * share, share, 1)
    ready = lax.optimization_barrier((w_qkv, query, near, stats, scale, move, mine))
    w_qkv, query, near, stats, scale, move, mine = ready

    mixed, theirs = encoder(lengths, order, normed, near_rows, other_rows, w_qkv)
    mixed = jnp.concatenate([mixed, partner(theirs)], axis=1)
    near_mixed, other_mixed = gather_tensor(mixed)
    halves = jnp.stack([odd, 1 - odd])[None]
    embedded = embed(
        jnp.concatenate([order, halves]), near_mixed, other_mixed, gathered, out_row, mine
    )
    targets = (x - jnp.array(FROM, jnp.int32)) % NX * NC
    give = embed_context(targets + 1 - c, embedded, gathered, 0)
    keep = embed_context(targets + c, embedded, gathered, 0)
    context = reduce_tensor(keep, give).astype(BF)
    near_context, other_context = gather_tensor(context)
    result = joint(
        prompt_lengths,
        order,
        near_context,
        other_context,
        scale,
        move,
        gathered,
        text_row,
        query,
        near,
        stats,
    )
    result = tensor_exchange(result.reshape(ndev, tokens, local))
    return jnp.swapaxes(result, 0, 1).reshape(1, tokens, ndev * local)


def solution(mesh):
    fine = Mesh(mesh.devices.reshape(NY, NZ, NX, NC), DP + TENSOR)
    in_specs = (
        P(DP, None, None),
        P(DP),
        P(),
        P(DP, TENSOR),
        P(DP, TENSOR),
        P(DP, TENSOR),
        P(TENSOR, DP),
        P(TENSOR, DP),
        P(DP, None),
        P(DP, None),
        P(DP, TENSOR),
        P(DP, TENSOR),
        P(DP, TENSOR, None),
        P(DP, TENSOR, None),
        P(DP, TENSOR, None),
    )
    out_specs = P(DP, TENSOR, None)
    return jax.shard_map(
        per_device, mesh=fine, in_specs=in_specs, out_specs=out_specs, check_vma=False
    )
```

```python
import functools

import jax
import jax.numpy as jnp
from jax import lax
from jax.experimental import pallas as pl
from jax.experimental.pallas import tpu as pltpu
from jax.sharding import Mesh
from jax.sharding import PartitionSpec as P

HEAD = 64
EPS = 1e-06
NY, NZ, NX, NC = 4, 8, 4, 2
DP = ("y", "z")
TENSOR = ("x", "c")
WIDTH = 2432
PIECE = 76
PADDED = 80
BF = jnp.bfloat16
F32 = jnp.float32
BIG = 56 * 2**20


def shift(array, axis, size, step):
    return lax.ppermute(array, axis, [(i, (i + step) % size) for i in range(size)])


def gather_over_y(shard):
    half = shard.shape[0] // 2
    y = lax.axis_index("y")
    up, down = shift(shard, "y", NY, 1), shift(shard, "y", NY, -1)
    far = [shift(up[:half], "y", NY, 1), shift(down[half:], "y", NY, -1)]
    far = jnp.concatenate(far, axis=0)
    block = jnp.zeros((NY,) + shard.shape, shard.dtype)
    for step, piece in ((0, shard), (-1, up), (1, down), (2, far)):
        block = lax.dynamic_update_slice_in_dim(block, piece[None], (y + step) % NY, 0)
    return block


def gather_over_z(shard, later):
    z = lax.axis_index("z")
    forward, backward = shift(shard, "z", NZ, 1), shift(shard, "z", NZ, -1)
    forward, backward, *later = lax.optimization_barrier((forward, backward, *later))
    found = [(0, shard), (-1, forward), (1, backward)]
    for step in (2, 3, 4):
        forward = shift(forward, "z", NZ, 1)
        found.append((-step, forward))
        if step < 4:
            backward = shift(backward, "z", NZ, -1)
            found.append((step, backward))
    line = jnp.zeros((NZ,) + shard.shape, shard.dtype)
    for step, piece in found:
        line = lax.dynamic_update_slice_in_dim(line, piece[None], (z + step) % NZ, 0)
    return line, later


def share_y(block):
    return lax.all_to_all(
        jnp.broadcast_to(block[None], (NY,) + block.shape), "y", 0, 0, tiled=True
    )


def ring_over_z(block):
    def z_pair(ahead, behind):
        return shift(ahead, "z", NZ, 1), shift(behind, "z", NZ, -1)

    s1, t1 = z_pair(block, block)
    s2, t2 = z_pair(s1, t1)
    s3, t3 = z_pair(s2, t2)
    s4 = shift(s3[: NY // 2], "z", NZ, 1)
    t4 = shift(t3[NY // 2 :], "z", NZ, -1)
    last = jnp.concatenate([s4, t4], axis=0)
    return [(0, block), (-1, s1), (1, t1), (-2, s2), (2, t2), (-3, s3), (3, t3), (4, last)]


def place_z(ring, split):
    z = lax.axis_index("z")
    pieces = [(step, split(block)) for step, block in ring]
    whole = jnp.zeros((NY, NZ) + pieces[0][1].shape[1:], pieces[0][1].dtype)
    for step, piece in pieces:
        whole = lax.dynamic_update_slice_in_dim(whole, piece[:, None], (z + step) % NZ, 1)
    return whole


def columns_to_devices(out_w):
    pairs = []
    for y in range(NY):
        for z in range(NZ):
            for x in range(NX):
                for c in range(NC):
                    source = ((x * NZ + 4 * c + z // 2) * NX + y) * NC + z % 2
                    pairs.append((source, ((y * NZ + z) * NX + x) * NC + c))
    return lax.ppermute(out_w, DP + TENSOR, pairs)


def pack_kernel(context_ref, key_w_ref, value_w_ref, moved_ref, out_ref, spare_ref, flat_ref):
    row = 0
    spare_ref[...] = jnp.zeros_like(spare_ref)
    spare_ref[:PIECE] = context_ref[...].astype(F32)
    for n in range(0, spare_ref.shape[1], 128):
        out_ref[row : row + PADDED] = spare_ref[:, n : n + 128].astype(BF)
        row += PADDED
    flat_ref[...] = jnp.zeros_like(flat_ref)
    local = key_w_ref.shape[1]
    flat_ref[:PIECE, :local] = key_w_ref[...].astype(F32)
    flat_ref[:PIECE, local:] = value_w_ref[...].astype(F32)
    for n in range(0, 2 * local, 128):
        out_ref[row : row + PADDED] = flat_ref[:, n : n + 128].astype(BF)
        row += PADDED
    out_ref[row:] = moved_ref[...]


def pack(context_t, text_key_w, text_value_w, moved):
    cols = 2 * text_key_w.shape[1]
    rows = (context_t.shape[1] + cols) // 128 * PADDED + moved.shape[0]
    vmem = pl.BlockSpec(memory_space=pltpu.VMEM)
    return pl.pallas_call(
        pack_kernel,
        in_specs=[vmem] * 4,
        out_specs=vmem,
        out_shape=jax.ShapeDtypeStruct((rows, 128), BF),
        scratch_shapes=[
            pltpu.VMEM((PADDED, context_t.shape[1]), F32),
            pltpu.VMEM((PADDED, cols), F32),
        ],
        compiler_params=pltpu.CompilerParams(vmem_limit_bytes=40 * 2**20),
    )(context_t, text_key_w, text_value_w, moved)


def encoder_kernel(
    lengths_ref, order_ref, mine_ref, near_ref, other_ref, weights_ref, out_ref, theirs_ref, qkv_ref
):
    i = pl.program_id(0)
    slots, width = out_ref.shape
    some = slots // (NX * NC)

    @pl.when(i == 0)
    def _():
        qkv_ref[...] = jnp.zeros_like(qkv_ref)

    states = [mine_ref[...]] + [ref[r] for r in range(NX) for ref in (near_ref, other_ref)]
    _, steps, rows, _ = weights_ref.shape
    weights = [
        jnp.concatenate([weights_ref[0, k, n : n + 128] for n in range(0, rows, 128)], axis=1)
        for k in range(steps)
    ]
    qkv_ref[...] += jnp.dot(
        jnp.concatenate(states, axis=0),
        jnp.concatenate(weights, axis=0),
        preferred_element_type=F32,
    )

    @pl.when(i == pl.num_programs(0) - 1)
    def _():
        lane = lax.broadcasted_iota(jnp.int32, (slots, slots), 1)
        place = jnp.zeros((slots, slots), jnp.int32)
        for n in range(NX * NC):
            start = (order_ref[n // NC, n % NC] - n) * some
            place += jnp.where(lane // some == n, start, 0)
        for sample, ok in enumerate((lane < lengths_ref[0], lane + place < lengths_ref[1])):
            rows = slice(sample * slots, (sample + 1) * slots)
            results = []
            for h in range(width // HEAD):
                query, key, value = (
                    qkv_ref[rows, part * width + h * HEAD : part * width + (h + 1) * HEAD].astype(BF)
                    for part in range(3)
                )
                scores = lax.dot_general(
                    query, key, (((1,), (1,)), ((), ())), preferred_element_type=F32
                )
                scores = jnp.where(ok, scores, -jnp.inf)
                expo = jnp.exp(scores - jnp.max(scores, axis=-1, keepdims=True))
                total = jnp.sum(expo, axis=-1, keepdims=True)
                mixed = jnp.dot(expo.astype(BF), value, preferred_element_type=F32)
                results.append(mixed / total)
            mixed = jnp.concatenate(results, axis=1).astype(BF)
            if sample == 0:
                out_ref[...] = mixed
            else:
                for n in range(NX * NC):
                    at = pl.multiple_of(order_ref[n // NC, n % NC] * some, some)
                    theirs_ref[pl.ds(at, some)] = mixed[n * some : (n + 1) * some]


def encoder(lengths, order, mine, near, other, weights):
    slots, enc = mine.shape
    steps, _, cols, _ = weights.shape
    smem = pl.BlockSpec(memory_space=pltpu.SMEM)
    out = pl.BlockSpec((slots, cols // 3), lambda i: (0, 0))
    line = pl.BlockSpec(near.shape[:2] + (enc // steps,), lambda i: (0, 0, i))
    return pl.pallas_call(
        encoder_kernel,
        grid=(steps,),
        in_specs=[
            smem,
            smem,
            pl.BlockSpec((slots, enc // steps), lambda i: (0, i)),
            line,
            line,
            pl.BlockSpec((1,) + weights.shape[1:], lambda i: (i, 0, 0, 0)),
        ],
        out_specs=[out, out],
        out_shape=[jax.ShapeDtypeStruct((slots, cols // 3), BF)] * 2,
        scratch_shapes=[pltpu.VMEM((2 * slots, cols), F32)],
        compiler_params=pltpu.CompilerParams(vmem_limit_bytes=40 * 2**20),
        cost_estimate=pl.CostEstimate(
            flops=4 * slots * enc * cols,
            bytes_accessed=2 * enc * (2 * slots + cols),
            transcendentals=2 * slots * slots * cols // 3 // HEAD,
        ),
    )(lengths, order, mine, near, other, weights)


def context_kernel(
    out_row,
    rows_ref,
    table_ref,
    places_ref,
    near_ref,
    other_ref,
    mine_ref,
    gathered_ref,
    give_ref,
    keep_ref,
    out_w_ref,
    weights_ref,
    embedded_ref,
    sems,
):
    pieces, width, _ = out_w_ref.shape
    rows = weights_ref.shape[1]
    each = give_ref.shape[1]
    copies = [
        pltpu.make_async_copy(gathered_ref.at[:, pl.ds(out_row, width)], out_w_ref, sems.at[pieces])
    ]
    for n in range(pieces):
        source = gathered_ref.at[places_ref[n], pl.ds(0, rows)]
        copies.append(pltpu.make_async_copy(source, weights_ref.at[n], sems.at[n]))
    for copy in copies:
        copy.start()
    copies[0].wait()
    half = width // 2
    for n in range(mine_ref.shape[1] // 128):
        attn = 0
        for r in range(NX):
            for core, ref in ((0, near_ref), (1, other_ref)):
                at = rows_ref[r, core] // 2 * NZ + table_ref[2 * n + rows_ref[r, core] % 2]
                for part in range(2):
                    start = pl.multiple_of(rows_ref[NX, part] * half, half)
                    attn += jnp.dot(
                        ref[r, :, part * half : (part + 1) * half],
                        out_w_ref[at, pl.ds(start, half)],
                        preferred_element_type=F32,
                    )
        cols = slice(n * 128, (n + 1) * 128)
        embedded_ref[cols] = (mine_ref[:, cols].astype(F32) + attn).T.astype(BF)
    for copy in copies[1:]:
        copy.wait()
    for n, out_ref in ((0, give_ref), (pieces // 2, keep_ref)):
        weights = [
            jnp.concatenate(
                [weights_ref[n + k, at : at + PADDED] for at in range(0, rows, PADDED)], axis=1
            )
            for k in range(pieces // 2)
        ]
        part = jnp.dot(
            jnp.concatenate(weights, axis=0), embedded_ref[...], preferred_element_type=F32
        ).astype(BF)
        for k in range(pieces // 2):
            out_ref[k // each, k % each] = part[k * PADDED : (k + 1) * PADDED]


def embed_context(rows, table, places, near, other, mine, gathered, out_row):
    slots, share = mine.shape
    width = near.shape[2]
    pieces = gathered.shape[0]
    each = pieces // (NX * NC)
    out = jax.ShapeDtypeStruct((NX, each, PADDED, slots), BF)
    vmem = pl.BlockSpec(memory_space=pltpu.VMEM)
    smem = pl.BlockSpec(memory_space=pltpu.SMEM)
    return pl.pallas_call(
        functools.partial(context_kernel, out_row),
        in_specs=[smem] * 3 + [vmem] * 3 + [pl.BlockSpec(memory_space=pl.ANY)],
        out_specs=[vmem, vmem],
        out_shape=[out, out],
        scratch_shapes=[
            pltpu.VMEM((pieces, width, 128), BF),
            pltpu.VMEM((pieces, share // 128 * PADDED, 128), BF),
            pltpu.VMEM((share, slots), BF),
            pltpu.SemaphoreType.DMA((pieces + 1,)),
        ],
        compiler_params=pltpu.CompilerParams(vmem_limit_bytes=BIG),
        cost_estimate=pl.CostEstimate(
            flops=4 * slots * share * NX * width + 2 * pieces * PADDED * share * slots,
            bytes_accessed=pieces * (width + share // 128 * PADDED) * 256 + near.size * 4,
            transcendentals=0,
        ),
    )(rows, table, places, near, other, mine, gathered)


def spread_kernel(query_ref, key_ref, value_ref, out_ref):
    ndev, _, cols = out_ref.shape
    local = cols // 3
    for j in range(ndev):
        for n, ref in enumerate((query_ref, key_ref, value_ref)):
            out_ref[j, :, n * local : (n + 1) * local] = ref[:, j * local : (j + 1) * local]


def spread_image(query, key, value):
    ndev = NX * NC
    tokens, cols = query.shape
    vmem = pl.BlockSpec(memory_space=pltpu.VMEM)
    return pl.pallas_call(
        spread_kernel,
        in_specs=[vmem] * 3,
        out_specs=vmem,
        out_shape=jax.ShapeDtypeStruct((ndev, tokens, 3 * cols // ndev), BF),
        compiler_params=pltpu.CompilerParams(vmem_limit_bytes=40 * 2**20),
    )(query, key, value)


def image_kernel(image_ref, out_ref, stats_ref):
    local = out_ref.shape[1]
    stats_ref[...] = jnp.zeros_like(stats_ref)
    for h in range(local // HEAD):
        at = h * HEAD
        query = image_ref[:, at : at + HEAD]
        key = image_ref[:, local + at : local + at + HEAD]
        value = image_ref[:, 2 * local + at : 2 * local + at + HEAD]
        scores = lax.dot_general(query, key, (((1,), (1,)), ((), ())), preferred_element_type=F32)
        scores = scores * HEAD ** (-0.5)
        top = jnp.max(scores, axis=-1, keepdims=True)
        expo = jnp.exp(scores - top)
        out_ref[:, at : at + HEAD] = jnp.dot(expo.astype(BF), value, preferred_element_type=F32)
        stats_ref[:, 2 * h : 2 * h + 1] = top
        stats_ref[:, 2 * h + 1 : 2 * h + 2] = jnp.sum(expo, axis=-1, keepdims=True)


def attend_image(image):
    tokens, cols = image.shape
    vmem = pl.BlockSpec(memory_space=pltpu.VMEM)
    return pl.pallas_call(
        image_kernel,
        in_specs=[vmem],
        out_specs=[vmem, vmem],
        out_shape=[
            jax.ShapeDtypeStruct((tokens, cols // 3), F32),
            jax.ShapeDtypeStruct((tokens, 128), F32),
        ],
        compiler_params=pltpu.CompilerParams(vmem_limit_bytes=40 * 2**20),
        cost_estimate=pl.CostEstimate(
            flops=4 * tokens * tokens * cols // 3,
            bytes_accessed=tokens * cols * 6,
            transcendentals=tokens * tokens * cols // 3 // HEAD,
        ),
    )(image)


def joint_kernel(
    row,
    length_ref,
    order_ref,
    table_ref,
    near_ref,
    other_ref,
    scale_ref,
    shift_ref,
    gathered_ref,
    query_ref,
    image_ref,
    stats_ref,
    out_ref,
    text_ref,
    states_ref,
    sem,
):
    _, each, rows, slots = near_ref.shape
    local = out_ref.shape[1]
    pieces = states_ref.shape[0]
    copies = [
        pltpu.make_async_copy(
            gathered_ref.at[:, pl.ds(row + n * rows, rows)],
            text_ref.at[:, :, pl.ds(n * 128, 128)],
            sem.at[n],
        )
        for n in range(2 * local // 128)
    ]
    for copy in copies:
        copy.start()
    real = lax.broadcasted_iota(jnp.int32, (rows, slots), 0) < PIECE
    parts = [(r, core, k) for r in range(NX) for core in range(NC) for k in range(each)]

    def context(part):
        r, core, k = part
        return (near_ref, other_ref)[core][r, k].astype(F32)

    total = jnp.zeros((rows, slots), F32)
    for part in parts:
        total += context(part)
    mean = jnp.sum(total, axis=0, keepdims=True) / WIDTH
    square = jnp.zeros((rows, slots), F32)
    for part in parts:
        centered = context(part) - mean
        square += centered * centered
    square = jnp.where(real, square, 0.0)
    factor = lax.rsqrt(jnp.sum(square, axis=0, keepdims=True) / WIDTH + EPS)
    for part in parts:
        r, core, k = part
        at = order_ref[r, core] * each + k
        scale = 1.0 + jnp.concatenate([scale_ref[at]] * (slots // 128), axis=1)
        move = jnp.concatenate([shift_ref[at]] * (slots // 128), axis=1)
        modulated = (context(part) - mean) * factor * scale + move
        states_ref[at // NZ * NZ + table_ref[at % NZ]] = jnp.where(real, modulated, 0.0).astype(BF)
    for copy in copies:
        copy.wait()
    text = lax.dot_general(
        text_ref[...].reshape(pieces * rows, 2 * local),
        states_ref[...].reshape(pieces * rows, slots),
        (((0,), (0,)), ((), ())),
        preferred_element_type=F32,
    )
    text = text.astype(BF)
    tokens = query_ref.shape[0]
    ok = lax.broadcasted_iota(jnp.int32, (tokens, slots), 1) < length_ref[0]
    for h in range(local // HEAD):
        at = h * HEAD
        query = query_ref[:, at : at + HEAD]
        far = jnp.dot(query, text[at : at + HEAD], preferred_element_type=F32) * HEAD ** (-0.5)
        far = jnp.where(ok, far, -jnp.inf)
        near_top = stats_ref[:, 2 * h : 2 * h + 1]
        top = jnp.maximum(near_top, jnp.max(far, axis=-1, keepdims=True))
        less = jnp.exp(near_top - top)
        far = jnp.exp(far - top)
        sums = stats_ref[:, 2 * h + 1 : 2 * h + 2] * less + jnp.sum(far, axis=-1, keepdims=True)
        result = image_ref[:, at : at + HEAD] * less
        result += lax.dot_general(
            far.astype(BF),
            text[local + at : local + at + HEAD],
            (((1,), (1,)), ((), ())),
            preferred_element_type=F32,
        )
        out_ref[:, at : at + HEAD] = (result / sums).astype(BF)


def joint(length, order, table, near, other, scale, move, gathered, row, query, image, stats):
    _, each, rows, slots = near.shape
    tokens, local = query.shape
    pieces = gathered.shape[0]
    vmem = pl.BlockSpec(memory_space=pltpu.VMEM)
    smem = pl.BlockSpec(memory_space=pltpu.SMEM)
    return pl.pallas_call(
        functools.partial(joint_kernel, row),
        in_specs=[smem] * 3 + [vmem] * 4 + [pl.BlockSpec(memory_space=pl.ANY)] + [vmem] * 3,
        out_specs=vmem,
        out_shape=jax.ShapeDtypeStruct((tokens, local), BF),
        scratch_shapes=[
            pltpu.VMEM((pieces, rows, 2 * local), BF),
            pltpu.VMEM((pieces, rows, slots), BF),
            pltpu.SemaphoreType.DMA((2 * local // 128,)),
        ],
        compiler_params=pltpu.CompilerParams(vmem_limit_bytes=48 * 2**20),
        cost_estimate=pl.CostEstimate(
            flops=4 * pieces * rows * local * slots + 4 * tokens * slots * local,
            bytes_accessed=pieces * rows * 2 * (slots + 2 * local),
            transcendentals=tokens * slots * local // HEAD,
        ),
    )(length, order, table, near, other, scale, move, gathered, query, image, stats)


def tensor_exchange(array):
    return lax.all_to_all(array, TENSOR, 0, 0, tiled=True)


def take(array, index, axis=0):
    return lax.dynamic_index_in_dim(array, index, axis, keepdims=False)


def other_core(array):
    return shift(array, "c", NC, 1)


FROM = (0, -1, 1, 2)


def reduce_tensor(keep, give):
    chip = (keep.astype(F32) + other_core(give).astype(F32)).astype(keep.dtype)
    half = chip.shape[1] // 2
    far = [shift(chip[3, :half], "x", NX, 2), shift(chip[3, half:], "x", NX, -2)]
    near = [shift(chip[1], "x", NX, 1), shift(chip[2], "x", NX, -1)]
    total = chip[0].astype(F32) + near[0].astype(F32) + near[1].astype(F32)
    return total + jnp.concatenate(far, axis=0).astype(F32)


def gather_tensor(block):
    far = shift(block, "x", NX, 2)
    line = jnp.stack([block, shift(block, "x", NX, 1), shift(block, "x", NX, -1), far])
    return line, other_core(line)


def per_device(
    text_states,
    prompt_lengths,
    attn_gain,
    query_w,
    key_w,
    value_w,
    out_w,
    context_w,
    mod_scale,
    mod_shift,
    text_key_w,
    text_value_w,
    image_query,
    image_key,
    image_value,
):
    slots, enc = text_states.shape[1:]
    ndev = NX * NC
    pieces = NY * NZ
    me = lax.axis_index("x") * NC + lax.axis_index("c")
    width = query_w.shape[1]
    half = width // 2
    share = enc // ndev
    y, x, c = (lax.axis_index(name) for name in "yxc")
    chips = (x + jnp.array(FROM, jnp.int32)) % NX * NC
    order = jnp.stack([chips + c, chips + 1 - c], axis=1)
    moved = columns_to_devices(out_w)
    moved, query_w, key_w, value_w = lax.optimization_barrier((moved, query_w, key_w, value_w))
    packed = pack(context_w.T, text_key_w, text_value_w, moved)
    text_row = share // 128 * PADDED
    out_row = packed.shape[0] - out_w.shape[0]

    odd = y % 2

    def heads(start):
        return jnp.concatenate(
            [lax.dynamic_slice_in_dim(w, start, half, 1) for w in (query_w, key_w, value_w)], axis=0
        )

    same, swapped = heads(odd * half), heads((1 - odd) * half)
    up, down = shift(swapped, "y", NY, 1), shift(swapped, "y", NY, -1)
    across = shift(same, "y", NY, 2)
    f1, b1 = shift(packed, "z", NZ, 1), shift(packed, "z", NZ, -1)
    images = (image_query, image_key, image_value)
    ready = lax.optimization_barrier((up, down, across, f1, b1, *images))
    up, down, across, f1, b1, *images = ready
    image_query, image_key, image_value = images
    block = jnp.zeros((NY,) + same.shape, BF)
    for step, piece in ((0, same), (-1, up), (1, down), (2, across)):
        block = lax.dynamic_update_slice_in_dim(block, piece[None], (y + step) % NY, 0)

    def partner(array):
        return lax.ppermute(array, "y", [(i, i ^ 1) for i in range(NY)])

    flat = text_states[0].astype(F32)
    scale = lax.rsqrt(jnp.mean(flat * flat, axis=-1, keepdims=True) + EPS)
    normed = (flat * scale * attn_gain).astype(BF)
    some = slots // ndev
    rows = partner(lax.dynamic_slice_in_dim(normed, me * some, some, 0))
    lengths = jnp.concatenate([prompt_lengths, partner(prompt_lengths)])
    flat_block = block.reshape(-1, 128)
    split = flat_block.shape[0]
    a1 = shift(jnp.concatenate([flat_block, f1]), "z", NZ, 1)
    e1 = shift(jnp.concatenate([flat_block, b1]), "z", NZ, -1)
    nheads = image_query.shape[-1] // HEAD // ndev
    local = nheads * HEAD
    tokens = image_query.shape[1]
    image = tensor_exchange(spread_image(image_query[0], image_key[0], image_value[0]))
    image = image.reshape(ndev * tokens, 3 * local)
    a1, e1, rows, image = lax.optimization_barrier((a1, e1, rows, image))
    near_rows, other_rows = gather_tensor(rows)

    def place_y(gathered, parts):
        for step, part, at in parts:
            gathered = lax.dynamic_update_slice(gathered, part[None], ((y + step) % NY, at, 0, 0))
        return gathered

    def y_pair(ahead, behind):
        return shift(ahead, "y", NY, 1), shift(behind, "y", NY, -1)

    group = jnp.stack([a1[split:], f1, packed, b1, e1[split:]])
    a2, e2 = shift(a1, "z", NZ, 1), shift(e1, "z", NZ, -1)
    after, before = y_pair(group, group)
    a2, e2, after, before = lax.optimization_barrier((a2, e2, after, before))
    a3, e3 = shift(a2, "z", NZ, 1), shift(e2[:split], "z", NZ, -1)
    low, high = y_pair(after[:3], before[3:])
    a3, e3, low, high = lax.optimization_barrier((a3, e3, low, high))
    a4 = shift(a3[: split // 2], "z", NZ, 1)
    e4 = shift(e3[split // 2 :], "z", NZ, -1)
    tail = jnp.stack([a2[split:], e2[split:], a3[split:]])
    tail_after, tail_before = y_pair(tail, tail)
    a4, e4, tail_after, tail_before = lax.optimization_barrier((a4, e4, tail_after, tail_before))
    tail_low, tail_high = y_pair(tail_after[:1], tail_before[1:])
    gathered = jnp.zeros((NY, NZ) + packed.shape, BF)
    gathered = place_y(gathered, ((0, group, 0), (-1, after, 0), (1, before, 0)))
    gathered = place_y(gathered, ((2, low, 0), (2, high, 3), (0, tail, 5), (-1, tail_after, 5)))
    gathered = place_y(gathered, ((1, tail_before, 5), (2, tail_low, 5), (2, tail_high, 6)))
    gathered = gathered.reshape((NY * NZ,) + packed.shape)
    ring = [(0, flat_block), (-1, a1), (1, e1), (-2, a2), (2, e2), (-3, a3), (3, e3)]
    ring = [(step, part[:split]) for step, part in ring] + [(4, jnp.concatenate([a4, e4]))]
    w_qkv = place_z(ring, lambda part: part.reshape(block.shape))
    z = lax.axis_index("z")
    table = jnp.array([2, 3, 4, 6, 7, 5, 0, 1], jnp.int32)[(jnp.arange(NZ, dtype=jnp.int32) - z) % NZ]


    near, stats = attend_image(image)
    query = image[:, :local]

    def spaced(row):
        row = jnp.pad(row.reshape(pieces, PIECE), ((0, 0), (0, PADDED - PIECE)))
        return jnp.broadcast_to(row[:, :, None], (pieces, PADDED, 128))

    scale, move = spaced(mod_scale), spaced(mod_shift)
    mine = lax.dynamic_slice_in_dim(text_states[0], me * share, share, 1)
    w_qkv, scale, move, mine = lax.optimization_barrier((w_qkv, scale, move, mine))

    mixed, theirs = encoder(lengths, order, normed, near_rows, other_rows, w_qkv)
    mixed = jnp.concatenate([mixed, partner(theirs)], axis=1)
    near_mixed, other_mixed = gather_tensor(mixed)
    ready = lax.optimization_barrier((near_mixed, query, near, stats))
    near_mixed, query, near, stats = ready
    halves = jnp.stack([odd, 1 - odd])[None]
    targets = (x - jnp.array(FROM, jnp.int32)) % NX * NC
    devices = jnp.concatenate([targets + 1 - c, targets + c])
    each = pieces // ndev
    places = devices[:, None] * each + jnp.arange(each, dtype=jnp.int32)[None]
    places = (places // NZ * NZ + table[places % NZ]).reshape(-1)
    give, keep = embed_context(
        jnp.concatenate([order, halves]),
        table,
        places,
        near_mixed,
        other_mixed,
        mine,
        gathered,
        out_row,
    )
    context = reduce_tensor(keep, give).astype(BF)
    near_context, other_context = gather_tensor(context)
    result = joint(
        prompt_lengths,
        order,
        table,
        near_context,
        other_context,
        scale,
        move,
        gathered,
        text_row,
        query,
        near,
        stats,
    )
    result = tensor_exchange(result.reshape(ndev, tokens, local))
    return jnp.swapaxes(result, 0, 1).reshape(1, tokens, ndev * local)


def solution(mesh):
    fine = Mesh(mesh.devices.reshape(NY, NZ, NX, NC), DP + TENSOR)
    in_specs = (
        P(DP, None, None),
        P(DP),
        P(),
        P(DP, TENSOR),
        P(DP, TENSOR),
        P(DP, TENSOR),
        P(TENSOR, DP),
        P(TENSOR, DP),
        P(DP, None),
        P(DP, None),
        P(DP, TENSOR),
        P(DP, TENSOR),
        P(DP, TENSOR, None),
        P(DP, TENSOR, None),
        P(DP, TENSOR, None),
    )
    out_specs = P(DP, TENSOR, None)
    return jax.shard_map(
        per_device, mesh=fine, in_specs=in_specs, out_specs=out_specs, check_vma=False
    )
```

```python
import functools

import jax
import jax.numpy as jnp
from jax import lax
from jax.experimental import pallas as pl
from jax.experimental.pallas import tpu as pltpu
from jax.sharding import Mesh
from jax.sharding import PartitionSpec as P

HEAD = 64
EPS = 1e-06
NY, NZ, NX, NC = 4, 8, 4, 2
DP = ("y", "z")
TENSOR = ("x", "c")
WIDTH = 2432
PIECE = 76
PADDED = 80
BF = jnp.bfloat16
F32 = jnp.float32
BIG = 40 * 2**20


def shift(array, axis, size, step):
    return lax.ppermute(array, axis, [(i, (i + step) % size) for i in range(size)])


def gather_over_y(shard):
    half = shard.shape[0] // 2
    y = lax.axis_index("y")
    up, down = shift(shard, "y", NY, 1), shift(shard, "y", NY, -1)
    far = [shift(up[:half], "y", NY, 1), shift(down[half:], "y", NY, -1)]
    far = jnp.concatenate(far, axis=0)
    block = jnp.zeros((NY,) + shard.shape, shard.dtype)
    for step, piece in ((0, shard), (-1, up), (1, down), (2, far)):
        block = lax.dynamic_update_slice_in_dim(block, piece[None], (y + step) % NY, 0)
    return block


def gather_over_z(shard, later):
    z = lax.axis_index("z")
    forward, backward = shift(shard, "z", NZ, 1), shift(shard, "z", NZ, -1)
    forward, backward, *later = lax.optimization_barrier((forward, backward, *later))
    found = [(0, shard), (-1, forward), (1, backward)]
    for step in (2, 3, 4):
        forward = shift(forward, "z", NZ, 1)
        found.append((-step, forward))
        if step < 4:
            backward = shift(backward, "z", NZ, -1)
            found.append((step, backward))
    line = jnp.zeros((NZ,) + shard.shape, shard.dtype)
    for step, piece in found:
        line = lax.dynamic_update_slice_in_dim(line, piece[None], (z + step) % NZ, 0)
    return line, later


def share_y(block):
    return lax.all_to_all(
        jnp.broadcast_to(block[None], (NY,) + block.shape), "y", 0, 0, tiled=True
    )


def ring_over_z(block):
    def z_pair(ahead, behind):
        return shift(ahead, "z", NZ, 1), shift(behind, "z", NZ, -1)

    s1, t1 = z_pair(block, block)
    s2, t2 = z_pair(s1, t1)
    s3, t3 = z_pair(s2, t2)
    s4 = shift(s3[: NY // 2], "z", NZ, 1)
    t4 = shift(t3[NY // 2 :], "z", NZ, -1)
    last = jnp.concatenate([s4, t4], axis=0)
    return [(0, block), (-1, s1), (1, t1), (-2, s2), (2, t2), (-3, s3), (3, t3), (4, last)]


def place_z(ring, split):
    z = lax.axis_index("z")
    pieces = [(step, split(block)) for step, block in ring]
    whole = jnp.zeros((NY, NZ) + pieces[0][1].shape[1:], pieces[0][1].dtype)
    for step, piece in pieces:
        whole = lax.dynamic_update_slice_in_dim(whole, piece[:, None], (z + step) % NZ, 1)
    return whole


def columns_to_devices(out_w):
    pairs = []
    for y in range(NY):
        for z in range(NZ):
            for x in range(NX):
                for c in range(NC):
                    source = ((x * NZ + 4 * c + z // 2) * NX + y) * NC + z % 2
                    pairs.append((source, ((y * NZ + z) * NX + x) * NC + c))
    return lax.ppermute(out_w, DP + TENSOR, pairs)


def pack_kernel(context_ref, key_w_ref, value_w_ref, moved_ref, out_ref, spare_ref, flat_ref):
    row = 0
    spare_ref[...] = jnp.zeros_like(spare_ref)
    spare_ref[:PIECE] = context_ref[...].astype(F32)
    for n in range(0, spare_ref.shape[1], 128):
        out_ref[row : row + PADDED] = spare_ref[:, n : n + 128].astype(BF)
        row += PADDED
    flat_ref[...] = jnp.zeros_like(flat_ref)
    local = key_w_ref.shape[1]
    flat_ref[:PIECE, :local] = key_w_ref[...].astype(F32)
    flat_ref[:PIECE, local:] = value_w_ref[...].astype(F32)
    for n in range(0, 2 * local, 128):
        out_ref[row : row + PADDED] = flat_ref[:, n : n + 128].astype(BF)
        row += PADDED
    out_ref[row:] = moved_ref[...]


def pack(context_t, text_key_w, text_value_w, moved):
    cols = 2 * text_key_w.shape[1]
    rows = (context_t.shape[1] + cols) // 128 * PADDED + moved.shape[0]
    vmem = pl.BlockSpec(memory_space=pltpu.VMEM)
    return pl.pallas_call(
        pack_kernel,
        in_specs=[vmem] * 4,
        out_specs=vmem,
        out_shape=jax.ShapeDtypeStruct((rows, 128), BF),
        scratch_shapes=[
            pltpu.VMEM((PADDED, context_t.shape[1]), F32),
            pltpu.VMEM((PADDED, cols), F32),
        ],
        compiler_params=pltpu.CompilerParams(vmem_limit_bytes=40 * 2**20),
    )(context_t, text_key_w, text_value_w, moved)


def encoder_kernel(
    lengths_ref, order_ref, mine_ref, near_ref, other_ref, weights_ref, out_ref, theirs_ref, qkv_ref
):
    i = pl.program_id(0)
    slots, width = out_ref.shape
    some = slots // (NX * NC)

    @pl.when(i == 0)
    def _():
        qkv_ref[...] = jnp.zeros_like(qkv_ref)

    states = [mine_ref[...]] + [ref[r] for r in range(NX) for ref in (near_ref, other_ref)]
    _, steps, rows, _ = weights_ref.shape
    weights = [
        jnp.concatenate([weights_ref[0, k, n : n + 128] for n in range(0, rows, 128)], axis=1)
        for k in range(steps)
    ]
    qkv_ref[...] += jnp.dot(
        jnp.concatenate(states, axis=0),
        jnp.concatenate(weights, axis=0),
        preferred_element_type=F32,
    )

    @pl.when(i == pl.num_programs(0) - 1)
    def _():
        lane = lax.broadcasted_iota(jnp.int32, (slots, slots), 1)
        place = jnp.zeros((slots, slots), jnp.int32)
        for n in range(NX * NC):
            start = (order_ref[n // NC, n % NC] - n) * some
            place += jnp.where(lane // some == n, start, 0)
        for sample, ok in enumerate((lane < lengths_ref[0], lane + place < lengths_ref[1])):
            rows = slice(sample * slots, (sample + 1) * slots)
            results = []
            for h in range(width // HEAD):
                query, key, value = (
                    qkv_ref[rows, part * width + h * HEAD : part * width + (h + 1) * HEAD].astype(BF)
                    for part in range(3)
                )
                scores = lax.dot_general(
                    query, key, (((1,), (1,)), ((), ())), preferred_element_type=F32
                )
                scores = jnp.where(ok, scores, -jnp.inf)
                expo = jnp.exp(scores - jnp.max(scores, axis=-1, keepdims=True))
                total = jnp.sum(expo, axis=-1, keepdims=True)
                mixed = jnp.dot(expo.astype(BF), value, preferred_element_type=F32)
                results.append(mixed / total)
            mixed = jnp.concatenate(results, axis=1).astype(BF)
            if sample == 0:
                out_ref[...] = mixed
            else:
                for n in range(NX * NC):
                    at = pl.multiple_of(order_ref[n // NC, n % NC] * some, some)
                    theirs_ref[pl.ds(at, some)] = mixed[n * some : (n + 1) * some]


def encoder(lengths, order, mine, near, other, weights):
    slots, enc = mine.shape
    steps, _, cols, _ = weights.shape
    smem = pl.BlockSpec(memory_space=pltpu.SMEM)
    out = pl.BlockSpec((slots, cols // 3), lambda i: (0, 0))
    line = pl.BlockSpec(near.shape[:2] + (enc // steps,), lambda i: (0, 0, i))
    return pl.pallas_call(
        encoder_kernel,
        grid=(steps,),
        in_specs=[
            smem,
            smem,
            pl.BlockSpec((slots, enc // steps), lambda i: (0, i)),
            line,
            line,
            pl.BlockSpec((1,) + weights.shape[1:], lambda i: (i, 0, 0, 0)),
        ],
        out_specs=[out, out],
        out_shape=[jax.ShapeDtypeStruct((slots, cols // 3), BF)] * 2,
        scratch_shapes=[pltpu.VMEM((2 * slots, cols), F32)],
        compiler_params=pltpu.CompilerParams(vmem_limit_bytes=40 * 2**20),
        cost_estimate=pl.CostEstimate(
            flops=4 * slots * enc * cols,
            bytes_accessed=2 * enc * (2 * slots + cols),
            transcendentals=2 * slots * slots * cols // 3 // HEAD,
        ),
    )(lengths, order, mine, near, other, weights)


def context_kernel(
    out_row,
    rows_ref,
    table_ref,
    places_ref,
    near_ref,
    other_ref,
    mine_ref,
    gathered_ref,
    give_ref,
    keep_ref,
    out_w_ref,
    weights_ref,
    embedded_ref,
    sems,
):
    pieces, width, _ = out_w_ref.shape
    rows = weights_ref.shape[1]
    each = give_ref.shape[1]
    copies = [
        pltpu.make_async_copy(gathered_ref.at[:, pl.ds(out_row, width)], out_w_ref, sems.at[pieces])
    ]
    for n in range(pieces):
        source = gathered_ref.at[places_ref[n], pl.ds(0, rows)]
        copies.append(pltpu.make_async_copy(source, weights_ref.at[n], sems.at[n]))
    for copy in copies:
        copy.start()
    copies[0].wait()
    half = width // 2
    for n in range(mine_ref.shape[1] // 128):
        attn = 0
        for r in range(NX):
            for core, ref in ((0, near_ref), (1, other_ref)):
                at = rows_ref[r, core] // 2 * NZ + table_ref[2 * n + rows_ref[r, core] % 2]
                for part in range(2):
                    start = pl.multiple_of(rows_ref[NX, part] * half, half)
                    attn += jnp.dot(
                        ref[r, :, part * half : (part + 1) * half],
                        out_w_ref[at, pl.ds(start, half)],
                        preferred_element_type=F32,
                    )
        cols = slice(n * 128, (n + 1) * 128)
        embedded_ref[cols] = (mine_ref[:, cols].astype(F32) + attn).T.astype(BF)
    for copy in copies[1:]:
        copy.wait()
    for n, out_ref in ((0, give_ref), (pieces // 2, keep_ref)):
        weights = [
            jnp.concatenate(
                [weights_ref[n + k, at : at + PADDED] for at in range(0, rows, PADDED)], axis=1
            )
            for k in range(pieces // 2)
        ]
        part = jnp.dot(
            jnp.concatenate(weights, axis=0), embedded_ref[...], preferred_element_type=F32
        ).astype(BF)
        for k in range(pieces // 2):
            out_ref[k // each, k % each] = part[k * PADDED : (k + 1) * PADDED]


def embed_context(rows, table, places, near, other, mine, gathered, out_row):
    slots, share = mine.shape
    width = near.shape[2]
    pieces = gathered.shape[0]
    each = pieces // (NX * NC)
    out = jax.ShapeDtypeStruct((NX, each, PADDED, slots), BF)
    vmem = pl.BlockSpec(memory_space=pltpu.VMEM)
    smem = pl.BlockSpec(memory_space=pltpu.SMEM)
    return pl.pallas_call(
        functools.partial(context_kernel, out_row),
        in_specs=[smem] * 3 + [vmem] * 3 + [pl.BlockSpec(memory_space=pl.ANY)],
        out_specs=[vmem, vmem],
        out_shape=[out, out],
        scratch_shapes=[
            pltpu.VMEM((pieces, width, 128), BF),
            pltpu.VMEM((pieces, share // 128 * PADDED, 128), BF),
            pltpu.VMEM((share, slots), BF),
            pltpu.SemaphoreType.DMA((pieces + 1,)),
        ],
        compiler_params=pltpu.CompilerParams(vmem_limit_bytes=BIG),
        cost_estimate=pl.CostEstimate(
            flops=4 * slots * share * NX * width + 2 * pieces * PADDED * share * slots,
            bytes_accessed=pieces * (width + share // 128 * PADDED) * 256 + near.size * 4,
            transcendentals=0,
        ),
    )(rows, table, places, near, other, mine, gathered)


def spread_kernel(query_ref, key_ref, value_ref, out_ref):
    ndev, _, cols = out_ref.shape
    local = cols // 3
    for j in range(ndev):
        for n, ref in enumerate((query_ref, key_ref, value_ref)):
            out_ref[j, :, n * local : (n + 1) * local] = ref[:, j * local : (j + 1) * local]


def spread_image(query, key, value):
    ndev = NX * NC
    tokens, cols = query.shape
    vmem = pl.BlockSpec(memory_space=pltpu.VMEM)
    return pl.pallas_call(
        spread_kernel,
        in_specs=[vmem] * 3,
        out_specs=vmem,
        out_shape=jax.ShapeDtypeStruct((ndev, tokens, 3 * cols // ndev), BF),
        compiler_params=pltpu.CompilerParams(vmem_limit_bytes=40 * 2**20),
    )(query, key, value)


def image_kernel(image_ref, out_ref, stats_ref):
    local = out_ref.shape[1]
    stats_ref[...] = jnp.zeros_like(stats_ref)
    for h in range(local // HEAD):
        at = h * HEAD
        query = image_ref[:, at : at + HEAD]
        key = image_ref[:, local + at : local + at + HEAD]
        value = image_ref[:, 2 * local + at : 2 * local + at + HEAD]
        scores = lax.dot_general(query, key, (((1,), (1,)), ((), ())), preferred_element_type=F32)
        scores = scores * HEAD ** (-0.5)
        top = jnp.max(scores, axis=-1, keepdims=True)
        expo = jnp.exp(scores - top)
        out_ref[:, at : at + HEAD] = jnp.dot(expo.astype(BF), value, preferred_element_type=F32)
        stats_ref[:, 2 * h : 2 * h + 1] = top
        stats_ref[:, 2 * h + 1 : 2 * h + 2] = jnp.sum(expo, axis=-1, keepdims=True)


def attend_image(image):
    tokens, cols = image.shape
    vmem = pl.BlockSpec(memory_space=pltpu.VMEM)
    return pl.pallas_call(
        image_kernel,
        in_specs=[vmem],
        out_specs=[vmem, vmem],
        out_shape=[
            jax.ShapeDtypeStruct((tokens, cols // 3), F32),
            jax.ShapeDtypeStruct((tokens, 128), F32),
        ],
        compiler_params=pltpu.CompilerParams(vmem_limit_bytes=40 * 2**20),
        cost_estimate=pl.CostEstimate(
            flops=4 * tokens * tokens * cols // 3,
            bytes_accessed=tokens * cols * 6,
            transcendentals=tokens * tokens * cols // 3 // HEAD,
        ),
    )(image)


def joint_kernel(
    row,
    length_ref,
    order_ref,
    table_ref,
    near_ref,
    other_ref,
    scale_ref,
    shift_ref,
    gathered_ref,
    query_ref,
    image_ref,
    stats_ref,
    out_ref,
    text_ref,
    states_ref,
    sem,
):
    _, each, rows, slots = near_ref.shape
    local = out_ref.shape[1]
    pieces = states_ref.shape[0]
    copies = [
        pltpu.make_async_copy(
            gathered_ref.at[:, pl.ds(row + n * rows, rows)],
            text_ref.at[:, :, pl.ds(n * 128, 128)],
            sem.at[n],
        )
        for n in range(2 * local // 128)
    ]
    for copy in copies:
        copy.start()
    real = lax.broadcasted_iota(jnp.int32, (rows, slots), 0) < PIECE
    parts = [(r, core, k) for r in range(NX) for core in range(NC) for k in range(each)]

    def context(part):
        r, core, k = part
        return (near_ref, other_ref)[core][r, k].astype(F32)

    total = jnp.zeros((rows, slots), F32)
    for part in parts:
        total += context(part)
    mean = jnp.sum(total, axis=0, keepdims=True) / WIDTH
    square = jnp.zeros((rows, slots), F32)
    for part in parts:
        centered = context(part) - mean
        square += centered * centered
    square = jnp.where(real, square, 0.0)
    factor = lax.rsqrt(jnp.sum(square, axis=0, keepdims=True) / WIDTH + EPS)
    for part in parts:
        r, core, k = part
        at = order_ref[r, core] * each + k
        scale = 1.0 + jnp.concatenate([scale_ref[at]] * (slots // 128), axis=1)
        move = jnp.concatenate([shift_ref[at]] * (slots // 128), axis=1)
        modulated = (context(part) - mean) * factor * scale + move
        states_ref[at // NZ * NZ + table_ref[at % NZ]] = jnp.where(real, modulated, 0.0).astype(BF)
    for copy in copies:
        copy.wait()
    text = lax.dot_general(
        text_ref[...].reshape(pieces * rows, 2 * local),
        states_ref[...].reshape(pieces * rows, slots),
        (((0,), (0,)), ((), ())),
        preferred_element_type=F32,
    )
    text = text.astype(BF)
    tokens = query_ref.shape[0]
    ok = lax.broadcasted_iota(jnp.int32, (tokens, slots), 1) < length_ref[0]
    for h in range(local // HEAD):
        at = h * HEAD
        query = query_ref[:, at : at + HEAD]
        far = jnp.dot(query, text[at : at + HEAD], preferred_element_type=F32) * HEAD ** (-0.5)
        far = jnp.where(ok, far, -jnp.inf)
        near_top = stats_ref[:, 2 * h : 2 * h + 1]
        top = jnp.maximum(near_top, jnp.max(far, axis=-1, keepdims=True))
        less = jnp.exp(near_top - top)
        far = jnp.exp(far - top)
        sums = stats_ref[:, 2 * h + 1 : 2 * h + 2] * less + jnp.sum(far, axis=-1, keepdims=True)
        result = image_ref[:, at : at + HEAD] * less
        result += lax.dot_general(
            far.astype(BF),
            text[local + at : local + at + HEAD],
            (((1,), (1,)), ((), ())),
            preferred_element_type=F32,
        )
        out_ref[:, at : at + HEAD] = (result / sums).astype(BF)


def joint(length, order, table, near, other, scale, move, gathered, row, query, image, stats):
    _, each, rows, slots = near.shape
    tokens, local = query.shape
    pieces = gathered.shape[0]
    vmem = pl.BlockSpec(memory_space=pltpu.VMEM)
    smem = pl.BlockSpec(memory_space=pltpu.SMEM)
    return pl.pallas_call(
        functools.partial(joint_kernel, row),
        in_specs=[smem] * 3 + [vmem] * 4 + [pl.BlockSpec(memory_space=pl.ANY)] + [vmem] * 3,
        out_specs=vmem,
        out_shape=jax.ShapeDtypeStruct((tokens, local), BF),
        scratch_shapes=[
            pltpu.VMEM((pieces, rows, 2 * local), BF),
            pltpu.VMEM((pieces, rows, slots), BF),
            pltpu.SemaphoreType.DMA((2 * local // 128,)),
        ],
        compiler_params=pltpu.CompilerParams(vmem_limit_bytes=48 * 2**20),
        cost_estimate=pl.CostEstimate(
            flops=4 * pieces * rows * local * slots + 4 * tokens * slots * local,
            bytes_accessed=pieces * rows * 2 * (slots + 2 * local),
            transcendentals=tokens * slots * local // HEAD,
        ),
    )(length, order, table, near, other, scale, move, gathered, query, image, stats)


def tensor_exchange(array):
    return lax.all_to_all(array, TENSOR, 0, 0, tiled=True)


def take(array, index, axis=0):
    return lax.dynamic_index_in_dim(array, index, axis, keepdims=False)


def other_core(array):
    return shift(array, "c", NC, 1)


FROM = (0, -1, 1, 2)


def reduce_tensor(keep, give):
    chip = (keep.astype(F32) + other_core(give).astype(F32)).astype(keep.dtype)
    half = chip.shape[1] // 2
    far = [shift(chip[3, :half], "x", NX, 2), shift(chip[3, half:], "x", NX, -2)]
    near = [shift(chip[1], "x", NX, 1), shift(chip[2], "x", NX, -1)]
    total = chip[0].astype(F32) + near[0].astype(F32) + near[1].astype(F32)
    return total + jnp.concatenate(far, axis=0).astype(F32)


def gather_tensor(block):
    far = shift(block, "x", NX, 2)
    line = jnp.stack([block, shift(block, "x", NX, 1), shift(block, "x", NX, -1), far])
    return line, other_core(line)


def per_device(
    text_states,
    prompt_lengths,
    attn_gain,
    query_w,
    key_w,
    value_w,
    out_w,
    context_w,
    mod_scale,
    mod_shift,
    text_key_w,
    text_value_w,
    image_query,
    image_key,
    image_value,
):
    slots, enc = text_states.shape[1:]
    ndev = NX * NC
    pieces = NY * NZ
    me = lax.axis_index("x") * NC + lax.axis_index("c")
    width = query_w.shape[1]
    half = width // 2
    share = enc // ndev
    y, x, c = (lax.axis_index(name) for name in "yxc")
    chips = (x + jnp.array(FROM, jnp.int32)) % NX * NC
    order = jnp.stack([chips + c, chips + 1 - c], axis=1)
    moved = columns_to_devices(out_w)
    moved, query_w, key_w, value_w = lax.optimization_barrier((moved, query_w, key_w, value_w))
    packed = pack(context_w.T, text_key_w, text_value_w, moved)
    text_row = share // 128 * PADDED
    out_row = packed.shape[0] - out_w.shape[0]

    odd = y % 2

    def heads(start):
        return jnp.concatenate(
            [lax.dynamic_slice_in_dim(w, start, half, 1) for w in (query_w, key_w, value_w)], axis=0
        )

    same, swapped = heads(odd * half), heads((1 - odd) * half)
    up, down = shift(swapped, "y", NY, 1), shift(swapped, "y", NY, -1)
    across = shift(same, "y", NY, 2)
    f1, b1 = shift(packed, "z", NZ, 1), shift(packed, "z", NZ, -1)
    images = (image_query, image_key, image_value)
    ready = lax.optimization_barrier((up, down, across, f1, b1, *images))
    up, down, across, f1, b1, *images = ready
    image_query, image_key, image_value = images
    block = jnp.zeros((NY,) + same.shape, BF)
    for step, piece in ((0, same), (-1, up), (1, down), (2, across)):
        block = lax.dynamic_update_slice_in_dim(block, piece[None], (y + step) % NY, 0)

    def partner(array):
        return lax.ppermute(array, "y", [(i, i ^ 1) for i in range(NY)])

    flat = text_states[0].astype(F32)
    scale = lax.rsqrt(jnp.mean(flat * flat, axis=-1, keepdims=True) + EPS)
    normed = (flat * scale * attn_gain).astype(BF)
    some = slots // ndev
    rows = partner(lax.dynamic_slice_in_dim(normed, me * some, some, 0))
    lengths = jnp.concatenate([prompt_lengths, partner(prompt_lengths)])
    flat_block = block.reshape(-1, 128)
    split = flat_block.shape[0]
    a1 = shift(jnp.concatenate([flat_block, f1]), "z", NZ, 1)
    e1 = shift(jnp.concatenate([flat_block, b1]), "z", NZ, -1)
    nheads = image_query.shape[-1] // HEAD // ndev
    local = nheads * HEAD
    tokens = image_query.shape[1]
    image = tensor_exchange(spread_image(image_query[0], image_key[0], image_value[0]))
    image = image.reshape(ndev * tokens, 3 * local)
    a1, e1, rows, image = lax.optimization_barrier((a1, e1, rows, image))
    near_rows, other_rows = gather_tensor(rows)

    def place_y(gathered, parts):
        for step, part, at in parts:
            gathered = lax.dynamic_update_slice(gathered, part[None], ((y + step) % NY, at, 0, 0))
        return gathered

    def y_pair(ahead, behind):
        return shift(ahead, "y", NY, 1), shift(behind, "y", NY, -1)

    group = jnp.stack([a1[split:], f1, packed, b1, e1[split:]])
    a2, e2 = shift(a1, "z", NZ, 1), shift(e1, "z", NZ, -1)
    after, before = y_pair(group, group)
    a2, e2, after, before = lax.optimization_barrier((a2, e2, after, before))
    a3, e3 = shift(a2, "z", NZ, 1), shift(e2[:split], "z", NZ, -1)
    low, high = y_pair(after[:3], before[3:])
    a3, e3, low, high = lax.optimization_barrier((a3, e3, low, high))
    a4 = shift(a3[: split // 2], "z", NZ, 1)
    e4 = shift(e3[split // 2 :], "z", NZ, -1)
    tail = jnp.stack([a2[split:], e2[split:], a3[split:]])
    tail_after, tail_before = y_pair(tail, tail)
    a4, e4, tail_after, tail_before = lax.optimization_barrier((a4, e4, tail_after, tail_before))
    tail_low, tail_high = y_pair(tail_after[:1], tail_before[1:])
    gathered = jnp.zeros((NY, NZ) + packed.shape, BF)
    gathered = place_y(gathered, ((0, group, 0), (-1, after, 0), (1, before, 0)))
    gathered = place_y(gathered, ((2, low, 0), (2, high, 3), (0, tail, 5), (-1, tail_after, 5)))
    gathered = place_y(gathered, ((1, tail_before, 5), (2, tail_low, 5), (2, tail_high, 6)))
    gathered = gathered.reshape((NY * NZ,) + packed.shape)
    ring = [(0, flat_block), (-1, a1), (1, e1), (-2, a2), (2, e2), (-3, a3), (3, e3)]
    ring = [(step, part[:split]) for step, part in ring] + [(4, jnp.concatenate([a4, e4]))]
    w_qkv = place_z(ring, lambda part: part.reshape(block.shape))
    z = lax.axis_index("z")
    table = jnp.array([2, 3, 4, 6, 7, 5, 0, 1], jnp.int32)[(jnp.arange(NZ, dtype=jnp.int32) - z) % NZ]


    near, stats = attend_image(image)
    query = image[:, :local]

    def spaced(row):
        row = jnp.pad(row.reshape(pieces, PIECE), ((0, 0), (0, PADDED - PIECE)))
        return jnp.broadcast_to(row[:, :, None], (pieces, PADDED, 128))

    scale, move = spaced(mod_scale), spaced(mod_shift)
    mine = lax.dynamic_slice_in_dim(text_states[0], me * share, share, 1)
    w_qkv, scale, move, mine = lax.optimization_barrier((w_qkv, scale, move, mine))

    mixed, theirs = encoder(lengths, order, normed, near_rows, other_rows, w_qkv)
    mixed = jnp.concatenate([mixed, partner(theirs)], axis=1)
    near_mixed, other_mixed = gather_tensor(mixed)
    ready = lax.optimization_barrier((near_mixed, query, near, stats))
    near_mixed, query, near, stats = ready
    halves = jnp.stack([odd, 1 - odd])[None]
    targets = (x - jnp.array(FROM, jnp.int32)) % NX * NC
    devices = jnp.concatenate([targets + 1 - c, targets + c])
    each = pieces // ndev
    places = devices[:, None] * each + jnp.arange(each, dtype=jnp.int32)[None]
    places = (places // NZ * NZ + table[places % NZ]).reshape(-1)
    give, keep = embed_context(
        jnp.concatenate([order, halves]),
        table,
        places,
        near_mixed,
        other_mixed,
        mine,
        gathered,
        out_row,
    )
    context = reduce_tensor(keep, give).astype(BF)
    near_context, other_context = gather_tensor(context)
    result = joint(
        prompt_lengths,
        order,
        table,
        near_context,
        other_context,
        scale,
        move,
        gathered,
        text_row,
        query,
        near,
        stats,
    )
    result = tensor_exchange(result.reshape(ndev, tokens, local))
    return jnp.swapaxes(result, 0, 1).reshape(1, tokens, ndev * local)


def solution(mesh):
    fine = Mesh(mesh.devices.reshape(NY, NZ, NX, NC), DP + TENSOR)
    in_specs = (
        P(DP, None, None),
        P(DP),
        P(),
        P(DP, TENSOR),
        P(DP, TENSOR),
        P(DP, TENSOR),
        P(TENSOR, DP),
        P(TENSOR, DP),
        P(DP, None),
        P(DP, None),
        P(DP, TENSOR),
        P(DP, TENSOR),
        P(DP, TENSOR, None),
        P(DP, TENSOR, None),
        P(DP, TENSOR, None),
    )
    out_specs = P(DP, TENSOR, None)
    return jax.shard_map(
        per_device, mesh=fine, in_specs=in_specs, out_specs=out_specs, check_vma=False
    )
```
